32 devices in a mesh: groups: 2 (over y), row: 4 (over z), tile: 4 (over x, core).
Axes of the slice: x: 2, y: 2, z: 4, core: 2. Of those that a mesh axis runs over, the one named last changes fastest.
Arguments:
- blocks: bfloat16 [512, 4, 128, 128], P(('groups', 'row', 'tile')), parts along dimension 0, may hold values from -0.4375 to 0.4375
- block_cols: int32 [512, 4], P(('groups', 'row')), parts along dimension 0, may hold values from -1 to 511, as said below
- pair_low: int32 [8], P('groups'), parts along dimension 0, may hold values from 0 to 248, as said below
Outputs:
- gram_band: float32 [8, 2048, 128], P(('groups', 'tile'), 'row'), parts along dimension 0
The draws below stay inside these ranges and needn't reach their ends.
There are 2 independent parts, one for each index of `groups`. The reference program is written for one: setup_inputs(seed, part) draws one part's arguments, and reference() takes and returns one part's arrays. A program takes and returns all parts, laid end to end along the dimension named above; each array names one. Nothing has to cross between parts.
Inputs may be any that keep to these rules, and one draw needn't show every extreme that they name: Entries are distinct multiples of 8; the partner block row of pair_low[p] is 511 - pair_low[p]. `block_cols`: in each panel the entries other than -1 are distinct and lie within 8 consecutive column blocks; each panel has at least two of them, and exactly one of them equals a block row of some pair (pair_low[p] or 511 - pair_low[p]). Among the 16 panels of one device (aligned blocks of 16 panels), exactly 4 hold a block row of a pair p with p = t, for each t from 0 to 3.
All inputs are finite; a program needn't handle non-finite values.
Results may differ from the reference program's by a relative error of at most 0.0003.
Values may be sent and summed in bfloat16 or wider, within the bound.
No kernel may reach another device: no remote copies, remote signals or barrier semaphores. Data moves between devices by JAX's collectives and lax.ppermute only.
A program may use at most 64 MiB of HBM per device.

```python
import jax
import jax.numpy as jnp
from jax import lax

NB = 512
BLK = 128
SPAN = 8
NNZ = 4
PAN_DEV = 16
PAIRS_DEV = 1
PANELS = 256
PAIRS = 4
N_ROW = 4
N_TILE = 4


def window_lows(key):
    choices_count = NB // (2 * SPAN)
    middle = (jax.random.permutation(key, choices_count - 2)[:PAIRS - 2] + 1).astype(jnp.int32)
    joined = jnp.concatenate([middle, jnp.array([0, choices_count - 1], jnp.int32)])
    return (jax.random.permutation(jax.random.fold_in(key, 1), joined) * SPAN).astype(jnp.int32)


def draw_pair_low(key, part):
    return window_lows(key)


def draw_block_cols(key, part):
    lowers = window_lows(key)
    key = jax.random.fold_in(key, 7)
    subkeys = jax.random.split(key, 7)
    device_count = PANELS // PAN_DEV
    panel_ids = jnp.arange(PAN_DEV, dtype=jnp.int32)[None, :]
    scores = jax.random.randint(subkeys[0], (device_count, PAN_DEV), 0, 2 ** 20) * PAN_DEV + panel_ids
    first_order = jnp.argsort(scores, axis=1, stable=True)
    order_rank = jnp.argsort(first_order, axis=1, stable=True).astype(jnp.int32)
    destination = (order_rank % N_TILE).reshape(PANELS)
    pair_index = destination * PAIRS_DEV + jax.random.randint(subkeys[1], (PANELS,), 0, PAIRS_DEV)
    upper_half = jax.random.randint(subkeys[2], (PANELS,), 0, 2)
    lowest_pair = jnp.argmin(lowers).astype(jnp.int32)
    lowest_owner = lowest_pair // PAIRS_DEV
    forced_panel = jnp.argmax(destination[:PAN_DEV] == lowest_owner).astype(jnp.int32)
    pair_index = pair_index.at[forced_panel].set(lowest_pair)
    upper_half = upper_half.at[forced_panel].set(1)
    pair_lower = lowers[pair_index]
    anchor = jnp.where(upper_half == 1, NB - 1 - pair_lower, pair_lower)
    root = jnp.clip(anchor - jax.random.randint(subkeys[3], (PANELS,), 0, SPAN), 0, NB - SPAN)
    offset = anchor - root
    span_ids = jnp.arange(SPAN, dtype=jnp.int32)[None, :]
    order_score = jax.random.randint(subkeys[4], (PANELS, SPAN), 0, 2 ** 20) * SPAN + span_ids
    order_score = jnp.where(span_ids == offset[:, None], -1, order_score)
    chosen = jnp.argsort(order_score, axis=1, stable=True)[:, :NNZ].astype(jnp.int32)
    live_count = jax.random.randint(subkeys[5], (PANELS, 1), 2, NNZ + 1)
    live_count = live_count.at[0, 0].set(2)
    slot_ids = jnp.arange(NNZ, dtype=jnp.int32)[None, :]
    columns = jnp.where(slot_ids < live_count, root[:, None] + chosen, -1)
    shuffle_score = jax.random.randint(subkeys[6], (PANELS, NNZ), 0, 2 ** 20) * NNZ + slot_ids
    reorder = jnp.argsort(shuffle_score, axis=1, stable=True)
    return jnp.take_along_axis(columns, reorder, axis=1).astype(jnp.int32)


def steps_of(stream_key, shape, shards, low, top_value):
    def one(dim, parts):
        steps = jax.random.uniform(jax.random.fold_in(jax.random.fold_in(stream_key, 6), dim), (parts,), jnp.float32, low / len(shards), top_value / len(shards))
        return jnp.repeat(jnp.exp(steps), shape[dim] // parts).reshape((-1,) + (1,) * (len(shape) - dim - 1))

    factor_of = one(*shards[0])
    for cut in shards[1:]:
        factor_of = factor_of * one(*cut)
    return factor_of


def scatter_about(rng, shape, scale, most, cuts=(), kind=jnp.bfloat16):
    loudness = steps_of(rng, shape, cuts, -0.22, 0.18) if cuts else 1.0
    values = jax.random.normal(rng, shape, jnp.float32) * scale * loudness
    return jnp.minimum(jnp.maximum(values, -most), most).astype(kind)


def setup_inputs(seed: int = 0, part: int = 0) -> dict:
    keys = jax.random.split(jax.random.key(seed), 4)
    part_keys = jax.random.split(jax.random.fold_in(keys[3], part), 4)
    blocks = scatter_about(part_keys[0], (PANELS, NNZ, BLK, BLK), 0.07, 0.4375, ((0, 16),))
    block_cols = draw_block_cols(jax.random.fold_in(jax.random.fold_in(keys[3], part), 71), part)
    pair_low = draw_pair_low(jax.random.fold_in(jax.random.fold_in(keys[3], part), 71), part)
    return {"blocks": blocks, "block_cols": block_cols, "pair_low": pair_low}


def reference(blocks, block_cols, pair_low):
    window = jnp.stack([pair_low, NB - 1 - pair_low], axis=1).reshape(-1).astype(jnp.int32)
    group_size = PANELS // N_ROW
    blocks_grouped = blocks.reshape(N_ROW, group_size, NNZ, BLK, BLK)
    cols_grouped = block_cols.reshape(N_ROW, group_size, NNZ)

    def one_row(target):
        def advance(summed, inputs):
            panel_blocks, panel_cols = inputs
            widened = panel_blocks.astype(jnp.float32)
            matches = (panel_cols == target).astype(jnp.float32)
            column = jnp.einsum('pj,pjrx->prx', matches, widened, precision=lax.Precision.HIGHEST)
            wanted = target - (SPAN - 1) + jnp.arange(SPAN, dtype=jnp.int32)
            places = ((panel_cols[:, :, None] == wanted[None, None, :]) & (panel_cols[:, :, None] >= 0)).astype(jnp.float32)
            products = jnp.einsum('prx,pjry->pjxy', column, widened, precision=lax.Precision.HIGHEST)
            return summed + jnp.einsum('pjs,pjxy->sxy', places, products, precision=lax.Precision.HIGHEST), None

        summed, unused = lax.scan(advance, jnp.zeros((SPAN, BLK, BLK), jnp.float32), (blocks_grouped, cols_grouped))
        return summed

    strips = lax.map(one_row, window).reshape(PAIRS, 2 * SPAN * BLK, BLK)
    row_ids = jnp.arange(2 * SPAN * BLK, dtype=jnp.int32)
    eye_mask = ((row_ids // BLK) % SPAN == SPAN - 1)[:, None] & ((row_ids % BLK)[:, None] == jnp.arange(BLK, dtype=jnp.int32)[None, :])
    return strips + eye_mask.astype(jnp.float32)[None]
```

```python
import functools

import jax
import jax.numpy as jnp
from jax import lax
from jax.experimental import pallas as pl
from jax.experimental.pallas import tpu as pltpu
from jax.sharding import PartitionSpec as P

NB = 512
SPAN = 8
STRIP = 2 * SPAN
TRASH = 2 * STRIP
EXTRA = 16

VMEM = pl.BlockSpec(memory_space=pltpu.VMEM)
SMEM = pl.BlockSpec(memory_space=pltpu.SMEM)
ANY = pl.BlockSpec(memory_space=pl.ANY)
PARAMS = pltpu.CompilerParams(vmem_limit_bytes=32 * 1024 * 1024)


def encode(block):
    top = jnp.max(jnp.abs(block), axis=0, keepdims=True)
    power = jnp.ceil(jnp.log2(jnp.maximum(top, 1e-30)))
    scaled = jnp.round(block * jnp.exp2(15.0 - power))
    codes = jnp.clip(scaled, -32767.0, 32767.0).astype(jnp.int32).astype(jnp.int16)
    return codes, power


def pack(blocks, message_ref, power_ref):
    size = blocks[0].shape[0]
    power_ref[...] = jnp.zeros_like(power_ref)
    for at, block in enumerate(blocks):
        codes, power = encode(block)
        message_ref[at * size : (at + 1) * size, :] = codes
        power_ref[at : at + 1, :] = power
    message_ref[len(blocks) * size :, :] = power_ref[...].astype(jnp.int32).astype(jnp.int16)


def powers_of(message_ref):
    rows = message_ref.shape[0]
    power = message_ref[rows - EXTRA :, :].astype(jnp.int32).astype(jnp.float32)
    return jnp.exp2(power - 15.0)


def unpack(message_ref, scales, at, size):
    codes = message_ref[at * size : (at + 1) * size, :].astype(jnp.int32).astype(jnp.float32)
    return codes * scales[at : at + 1, :]


def plan_kernel(panels_here, cols_ref, low_ref, plan_ref, count_ref):
    here = lax.axis_index("tile")
    for at in range(4):
        count_ref[at] = 0
    quota = panels_here // lax.axis_size("tile")

    def one(step, carry):
        mate = step // panels_here
        panel = step % panels_here
        row = (here ^ mate) * panels_here + panel
        cols = [cols_ref[row, slot] for slot in range(4)]
        tile = jnp.int32(0)
        slot_hit = jnp.int32(0)
        target = jnp.int32(0)
        for slot, col in enumerate(cols):
            folded = jnp.minimum(col, NB - 1 - col)
            for index in range(low_ref.shape[0]):
                hit = folded == low_ref[index]
                tile = jnp.where(hit, index, tile)
                slot_hit = jnp.where(hit, slot, slot_hit)
                target = jnp.where(hit, col, target)
        apart = tile ^ here
        half = jnp.where(target >= NB // 2, SPAN, 0)
        local = jnp.where(apart == 0, 1, 0)

        @pl.when((apart == 0) | (apart == 2))
        def _():
            group = local * 2 + mate
            entry = group * quota + count_ref[group]
            count_ref[group] = count_ref[group] + 1
            plan_ref[entry, 0] = panel
            plan_ref[entry, 1] = slot_hit
            for slot, col in enumerate(cols):
                place = col - target + SPAN - 1
                good = (col >= 0) & (place >= 0) & (place < SPAN)
                plan_ref[entry, 2 + slot] = jnp.where(good, local * STRIP + half + place, TRASH)

        return carry

    lax.fori_loop(0, 2 * panels_here, one, 0)


def products(plan_ref, own_ref, mate_ref, held, sums, sems):
    entries = held.shape[0]
    quota = entries // 4
    copies = []
    for entry in range(entries):
        source = mate_ref if entry // quota % 2 else own_ref
        copies.append(pltpu.make_async_copy(source.at[plan_ref[entry, 0]], held.at[entry], sems.at[entry]))
        copies[-1].start()
    sums[...] = jnp.zeros_like(sums)
    for entry in range(entries):
        copies[entry].wait()
        column = held[entry, plan_ref[entry, 1]]
        for slot in range(held.shape[1]):
            place = plan_ref[entry, 2 + slot]
            sums[place] += lax.dot_general(
                column, held[entry, slot], (((0,), (0,)), ((), ())), preferred_element_type=jnp.float32
            )


def split_kernel(plan_ref, own_ref, mate_ref, x_ref, z1_ref, z2_ref, z3_ref, keep_p, keep_q, held, sums, power, sems):
    products(plan_ref, own_ref, mate_ref, held, sums, sems)
    here = lax.axis_index("row")
    pack([sums[4 * owner + i] for owner in range(4) for i in range(2)], x_ref, power)
    for apart, z_ref in ((1, z1_ref), (2, z2_ref), (3, z3_ref)):
        first = 4 * (here ^ apart) + 2
        pack([sums[first], sums[first + 1], sums[STRIP + first], sums[STRIP + first + 1]], z_ref, power)
    for owner in range(4):
        for i in range(2):
            keep_p[2 * owner + i] = sums[STRIP + 4 * owner + i]
    for i in range(2):
        keep_q[i] = sums[4 * here + 2 + i]
        keep_q[2 + i] = sums[STRIP + 4 * here + 2 + i]


def after_x_kernel(keep_p, x_ref, z1_ref, z2_ref, z3_ref, own_ref, sums, power):
    here = lax.axis_index("row")
    size = keep_p.shape[1]
    scales = powers_of(x_ref)
    for at in range(keep_p.shape[0]):
        sums[at] = keep_p[at] + unpack(x_ref, scales, at, size)
    for apart, z_ref in ((1, z1_ref), (2, z2_ref), (3, z3_ref)):
        first = 2 * (here ^ apart)
        pack([sums[first], sums[first + 1]], z_ref, power)
    for i in range(2):
        own_ref[i] = sums[2 * here + i]


def after_z_kernel(keep_q, z1_ref, z2_ref, z3_ref, x_ref, own_ref, power):
    size = keep_q.shape[1]
    scales = [powers_of(ref) for ref in (z1_ref, z2_ref, z3_ref)]
    totals = []
    for at in range(4):
        total = keep_q[at]
        for ref, scale in zip((z1_ref, z2_ref, z3_ref), scales):
            total = total + unpack(ref, scale, at, size)
        totals.append(total)
    pack(totals[:2], x_ref, power)
    own_ref[0] = totals[2]
    own_ref[1] = totals[3]


def last_kernel(own_p, z1_ref, z2_ref, z3_ref, own_q, x_ref, out_ref):
    size = own_p.shape[1]
    odd = lax.axis_index("row") % 2
    scales = [powers_of(ref) for ref in (z1_ref, z2_ref, z3_ref)]
    for at in range(2):
        total = own_p[at]
        for ref, scale in zip((z1_ref, z2_ref, z3_ref), scales):
            total = total + unpack(ref, scale, at, size)
        out_ref[0, at * size : (at + 1) * size, :] = total
    scale = powers_of(x_ref)
    for at in range(2):
        total = own_q[at] + unpack(x_ref, scale, at, size)
        if at == 1:
            rows = lax.broadcasted_iota(jnp.int32, total.shape, 0)
            columns = lax.broadcasted_iota(jnp.int32, total.shape, 1)
            total = total + jnp.where((rows == columns) & (odd == 1), 1.0, 0.0)
        out_ref[0, (2 + at) * size : (3 + at) * size, :] = total


def full_kernel(plan_ref, own_ref, mate_ref, x_ref, keep_ref, held, sums, power, sems):
    products(plan_ref, own_ref, mate_ref, held, sums, sems)
    pack([sums[at] for at in range(STRIP)], x_ref, power)
    keep_ref[...] = sums[STRIP : 2 * STRIP]


def add_kernel(keep_ref, x_ref, sum_ref):
    size = keep_ref.shape[1]
    scales = powers_of(x_ref)
    for at in range(STRIP):
        sum_ref[at] = keep_ref[at] + unpack(x_ref, scales, at, size)


def call(kernel, outs, operands, specs, scratch=(), flops=0, size=1 << 20):
    return pl.pallas_call(
        kernel,
        out_shape=outs,
        in_specs=specs,
        out_specs=jax.tree.map(lambda _: VMEM, outs),
        scratch_shapes=list(scratch),
        compiler_params=PARAMS,
        cost_estimate=pl.CostEstimate(flops=flops, bytes_accessed=size, transcendentals=0),
    )(*operands)


def on_device(blocks, block_cols, pair_low):
    panels_here, slots, size, _ = blocks.shape
    tiles_count = lax.axis_size("tile")
    rows_count = lax.axis_size("row")
    assert tiles_count == 4 and pair_low.shape[0] == 4 and slots == 4
    entries = panels_here

    def swap(value, axis, apart):
        return lax.ppermute(value, axis, [(i, i ^ apart) for i in range(lax.axis_size(axis))])

    def message(count):
        return jax.ShapeDtypeStruct((count * size + EXTRA, size), jnp.int16)

    def full(count):
        return jax.ShapeDtypeStruct((count, size, size), jnp.float32)

    mate = swap(blocks, "tile", 1)
    plan = pl.pallas_call(
        functools.partial(plan_kernel, panels_here),
        out_shape=jax.ShapeDtypeStruct((entries, 8), jnp.int32),
        in_specs=[SMEM, SMEM],
        out_specs=SMEM,
        scratch_shapes=[pltpu.SMEM((4,), jnp.int32)],
        cost_estimate=pl.CostEstimate(flops=0, bytes_accessed=1 << 22, transcendentals=0),
    )(block_cols, pair_low)

    power = pltpu.VMEM((EXTRA, size), jnp.float32)
    scratch = [
        pltpu.VMEM((entries, slots, size, size), blocks.dtype),
        pltpu.VMEM((2 * STRIP + 1, size, size), jnp.float32),
        power,
        pltpu.SemaphoreType.DMA((entries,)),
    ]
    operands = (plan, blocks, mate)
    specs = [SMEM, ANY, ANY]

    if rows_count != 4:
        across, keep = call(full_kernel, [message(STRIP), full(STRIP)], operands, specs, scratch, 1 << 28, 4 << 20)
        strip = call(add_kernel, full(STRIP), (keep, swap(across, "tile", 2)), [VMEM, VMEM])
        share = lax.psum_scatter(strip.reshape(1, STRIP * size, size), "row", scatter_dimension=1, tiled=True)
        rows = lax.axis_index("row") * share.shape[1] + jnp.arange(share.shape[1], dtype=jnp.int32)
        unit = (rows // size % SPAN == SPAN - 1)[:, None] & ((rows % size)[:, None] == jnp.arange(size)[None, :])
        return share + unit.astype(jnp.float32)[None]

    x_p, q1, q2, q3, keep_p, keep_q = call(
        split_kernel,
        [message(8), message(4), message(4), message(4), full(8), full(4)],
        operands, specs, scratch, 1 << 28, 4 << 20,
    )
    q3 = swap(q3, "row", 3)
    q2 = swap(q2, "row", 2)
    x_p = swap(x_p, "tile", 2)
    q1 = swap(q1, "row", 1)
    p1, p2, p3, own_p = call(
        after_x_kernel, [message(2)] * 3 + [full(2)], (keep_p, x_p), [VMEM] * 2, [pltpu.VMEM((8, size, size), jnp.float32), power]
    )
    p3 = swap(p3, "row", 3)
    p2 = swap(p2, "row", 2)
    p1 = swap(p1, "row", 1)
    x_q, own_q = call(after_z_kernel, [message(2), full(2)], (keep_q, q1, q2, q3), [VMEM] * 4, [power])
    x_q = swap(x_q, "tile", 2)
    return call(
        last_kernel, jax.ShapeDtypeStruct((1, 4 * size, size), jnp.float32), (own_p, p1, p2, p3, own_q, x_q), [VMEM] * 6
    )


def solution(mesh):
    return jax.shard_map(
        on_device,
        mesh=mesh,
        in_specs=(
            P(("groups", "row", "tile"), None, None, None),
            P(("groups", "row"), None),
            P("groups"),
        ),
        out_specs=P(("groups", "tile"), "row", None),
        check_vma=False,
    )
```

```python
import jax
import jax.numpy as jnp
from jax import lax
from jax.experimental import pallas as pl
from jax.experimental.pallas import tpu as pltpu
from jax.sharding import PartitionSpec as P

NB = 512
SPAN = 8
STRIP = 2 * SPAN
EXTRA = 16

VMEM = pl.BlockSpec(memory_space=pltpu.VMEM)
SMEM = pl.BlockSpec(memory_space=pltpu.SMEM)
HBM = pl.BlockSpec(memory_space=pltpu.HBM)
PARAMS = pltpu.CompilerParams(vmem_limit_bytes=32 * 1024 * 1024)


def encode(block):
    top = jnp.max(jnp.abs(block), axis=0, keepdims=True)
    power = jnp.ceil(jnp.log2(jnp.maximum(top, 1e-30)))
    scaled = jnp.round(block * jnp.exp2(15.0 - power))
    codes = jnp.clip(scaled, -32767.0, 32767.0).astype(jnp.int32).astype(jnp.int16)
    return codes, power


def pack(blocks, message_ref, power_ref):
    size = blocks[0].shape[0]
    power_ref[...] = jnp.zeros_like(power_ref)
    for at, block in enumerate(blocks):
        codes, power = encode(block)
        message_ref[at * size : (at + 1) * size, :] = codes
        power_ref[at : at + 1, :] = power
    message_ref[len(blocks) * size :, :] = power_ref[...].astype(jnp.int32).astype(jnp.int16)


def powers_of(message_ref):
    rows = message_ref.shape[0]
    power = message_ref[rows - EXTRA :, :].astype(jnp.int32).astype(jnp.float32)
    return jnp.exp2(power - 15.0)


def unpack(message_ref, scales, at, size):
    codes = message_ref[at * size : (at + 1) * size, :].astype(jnp.int32).astype(jnp.float32)
    return codes * scales[at : at + 1, :]


def plan_of(cols_ref, low_ref, fields_ref, quota):
    here = lax.axis_index("tile")
    cols = cols_ref[...]
    count = cols.shape[1]
    folded = jnp.minimum(cols, NB - 1 - cols)
    near = (folded == low_ref[here]).astype(jnp.int32)
    far = (folded == low_ref[here ^ 2]).astype(jnp.int32)
    hit = near + far
    target = jnp.sum(hit * cols, axis=0, keepdims=True)
    slot = jnp.sum(hit * lax.broadcasted_iota(jnp.int32, cols.shape, 0), axis=0, keepdims=True)
    local = jnp.sum(near, axis=0, keepdims=True)
    wanted = jnp.sum(hit, axis=0, keepdims=True)
    place = cols - target + SPAN - 1
    good = (cols >= 0) & (place >= 0) & (place < SPAN)
    place = jnp.where(good, place + jnp.where(target >= NB // 2, SPAN, 0), STRIP)
    panel = lax.broadcasted_iota(jnp.int32, (1, count), 1)
    device = panel // (4 * quota)
    mate = (device == (here ^ 1)).astype(jnp.int32)
    wanted = (wanted > 0) & ((device == here) | (mate > 0))
    group = jnp.where(wanted, local * 2 + mate, -1)
    members = (lax.broadcasted_iota(jnp.int32, (8, count), 0) == group).astype(jnp.float32)
    before = (
        lax.broadcasted_iota(jnp.int32, (count, count), 0) < lax.broadcasted_iota(jnp.int32, (count, count), 1)
    ).astype(jnp.float32)
    ranks = jnp.dot(members, before, preferred_element_type=jnp.float32)
    rank = jnp.sum(members * ranks, axis=0, keepdims=True).astype(jnp.int32)
    entry = jnp.where(wanted, group * quota + rank, -1)
    chosen = (lax.broadcasted_iota(jnp.int32, (4 * quota, count), 0) == entry).astype(jnp.float32)
    fields_ref[...] = jnp.zeros_like(fields_ref)
    fields_ref[0:1, 0:count] = (panel % (4 * quota)).astype(jnp.float32)
    fields_ref[1:2, 0:count] = slot.astype(jnp.float32)
    fields_ref[2:6, 0:count] = place.astype(jnp.float32)
    table = lax.dot_general(
        chosen, fields_ref[:, 0:count], (((1,), (1,)), ((), ())), preferred_element_type=jnp.float32
    )
    return table.astype(jnp.int32)


def add_products(plan_ref, entry, panels_ref, sums_ref):
    panel = plan_ref[entry, 0]
    column = panels_ref[panel, plan_ref[entry, 1]].T
    size = column.shape[0]
    wide = jnp.concatenate([panels_ref[panel, slot] for slot in range(4)], axis=1)
    made = jnp.dot(column, wide, preferred_element_type=jnp.float32)
    for slot in range(4):
        sums_ref[plan_ref[entry, 2 + slot]] += made[:, slot * size : (slot + 1) * size]


def near_kernel(cols_hbm, low_hbm, blocks_ref, plan_ref, far_ref, own_ref, held, cols_ref, low_ref, fields, table, sems):
    quota = blocks_ref.shape[0] // 4
    cols_copy = pltpu.make_async_copy(cols_hbm, cols_ref, sems.at[0])
    low_copy = pltpu.make_async_copy(low_hbm, low_ref, sems.at[1])
    held_copy = pltpu.make_async_copy(blocks_ref, held, sems.at[2])
    cols_copy.start()
    low_copy.start()
    held_copy.start()
    far_ref[...] = jnp.zeros_like(far_ref)
    own_ref[...] = jnp.zeros_like(own_ref)
    low_copy.wait()
    cols_copy.wait()
    table[:, 0:8] = plan_of(cols_ref, low_ref, fields, quota)
    plan_copy = pltpu.make_async_copy(table, plan_ref, sems.at[3])
    plan_copy.start()
    plan_copy.wait()
    held_copy.wait()
    for at in range(quota):
        add_products(plan_ref, at, held, far_ref)
        add_products(plan_ref, 2 * quota + at, held, own_ref)


def add_mate(plan_ref, mate_ref, far_ref, own_ref):
    quota = mate_ref.shape[0] // 4
    for at in range(quota):
        add_products(plan_ref, quota + at, mate_ref, far_ref)
        add_products(plan_ref, 3 * quota + at, mate_ref, own_ref)


def split_kernel(plan_ref, mate_ref, far_in, own_in, z2_ref, z3_ref, z1_ref, x_ref, far_ref, own_ref, power):
    add_mate(plan_ref, mate_ref, far_ref, own_ref)
    here = lax.axis_index("row")
    for apart, z_ref in ((1, z1_ref), (2, z2_ref), (3, z3_ref)):
        first = 4 * (here ^ apart) + 2
        pack([far_ref[first], far_ref[first + 1], own_ref[first], own_ref[first + 1]], z_ref, power)
    pack([far_ref[4 * owner + i] for owner in range(4) for i in range(2)], x_ref, power)


def after_x_kernel(own_ref, x_ref, z2_ref, z3_ref, z1_ref, keep_ref, sums, power):
    here = lax.axis_index("row")
    size = own_ref.shape[1]
    scales = powers_of(x_ref)
    for owner in range(4):
        for i in range(2):
            at = 2 * owner + i
            sums[at] = own_ref[4 * owner + i] + unpack(x_ref, scales, at, size)
    for apart, z_ref in ((1, z1_ref), (2, z2_ref), (3, z3_ref)):
        first = 2 * (here ^ apart)
        pack([sums[first], sums[first + 1]], z_ref, power)
    for i in range(2):
        keep_ref[i] = sums[2 * here + i]


def after_z_kernel(after_ref, far_ref, own_ref, z2_ref, z3_ref, z1_ref, x_ref, keep_ref, power):
    here = lax.axis_index("row")
    size = own_ref.shape[1]
    scales = [powers_of(ref) for ref in (z1_ref, z2_ref, z3_ref)]
    totals = []
    for at in range(4):
        sums_ref = far_ref if at < 2 else own_ref
        total = sums_ref[4 * here + 2 + at % 2]
        for ref, scale in zip((z1_ref, z2_ref, z3_ref), scales):
            total = total + unpack(ref, scale, at, size)
        totals.append(total)
    pack(totals[:2], x_ref, power)
    keep_ref[0] = totals[2]
    keep_ref[1] = totals[3]


def last_kernel(own_p, z2_ref, z3_ref, z1_ref, own_q, x_ref, out_ref):
    size = own_p.shape[1]
    odd = lax.axis_index("row") % 2
    scales = [powers_of(ref) for ref in (z1_ref, z2_ref, z3_ref)]
    for at in range(2):
        total = own_p[at]
        for ref, scale in zip((z1_ref, z2_ref, z3_ref), scales):
            total = total + unpack(ref, scale, at, size)
        out_ref[0, at * size : (at + 1) * size, :] = total
    scale = powers_of(x_ref)
    for at in range(2):
        total = own_q[at] + unpack(x_ref, scale, at, size)
        if at == 1:
            rows = lax.broadcasted_iota(jnp.int32, total.shape, 0)
            columns = lax.broadcasted_iota(jnp.int32, total.shape, 1)
            total = total + jnp.where((rows == columns) & (odd == 1), 1.0, 0.0)
        out_ref[0, (2 + at) * size : (3 + at) * size, :] = total


def full_kernel(plan_ref, mate_ref, far_in, own_in, x_ref, far_ref, own_ref, power):
    add_mate(plan_ref, mate_ref, far_ref, own_ref)
    pack([far_ref[at] for at in range(STRIP)], x_ref, power)


def add_kernel(own_ref, x_ref, sum_ref):
    size = own_ref.shape[1]
    scales = powers_of(x_ref)
    for at in range(STRIP):
        sum_ref[at] = own_ref[at] + unpack(x_ref, scales, at, size)


def call(kernel, outs, operands, specs, out_specs=None, scratch=(), size=1 << 20, aliases=None):
    return pl.pallas_call(
        kernel,
        out_shape=outs,
        in_specs=specs,
        out_specs=jax.tree.map(lambda _: VMEM, outs) if out_specs is None else out_specs,
        scratch_shapes=list(scratch),
        input_output_aliases=aliases or {},
        compiler_params=PARAMS,
        cost_estimate=pl.CostEstimate(flops=0, bytes_accessed=size, transcendentals=0),
    )(*operands)


def on_device(blocks, block_cols, pair_low):
    panels_here, slots, size, _ = blocks.shape
    tiles_count = lax.axis_size("tile")
    rows_count = lax.axis_size("row")
    assert tiles_count == 4 and pair_low.shape[0] == 4 and slots == 4

    def swap(value, axis, apart):
        return lax.ppermute(value, axis, [(i, i ^ apart) for i in range(lax.axis_size(axis))])

    def message(count):
        return jax.ShapeDtypeStruct((count * size + EXTRA, size), jnp.int16)

    def full(count):
        return jax.ShapeDtypeStruct((count, size, size), jnp.float32)

    power = pltpu.VMEM((EXTRA, size), jnp.float32)
    mate = swap(blocks, "tile", 1)
    plan, far, own = call(
        near_kernel,
        [jax.ShapeDtypeStruct((panels_here, 128), jnp.int32), full(STRIP + 1), full(STRIP + 1)],
        tuple(pltpu.with_memory_space_constraint(value, pltpu.HBM) for value in (block_cols.T, pair_low, blocks)),
        [HBM, HBM, HBM],
        [SMEM, VMEM, VMEM],
        [
            pltpu.VMEM(blocks.shape, blocks.dtype),
            pltpu.VMEM(block_cols.shape[::-1], jnp.int32),
            pltpu.SMEM(pair_low.shape, jnp.int32),
            pltpu.VMEM((8, 128), jnp.float32),
            pltpu.VMEM((panels_here, 128), jnp.int32),
            pltpu.SemaphoreType.DMA((4,)),
        ],
        8 << 20,
    )
    operands = (plan, mate, far, own)
    specs = [SMEM, VMEM, VMEM, VMEM]

    if rows_count != 4:
        across, far, own = call(
            full_kernel, [message(STRIP), far, own], operands, specs, scratch=[power], aliases={2: 1, 3: 2}
        )
        strip = call(add_kernel, full(STRIP), (own, swap(across, "tile", 2)), [VMEM, VMEM])
        share = lax.psum_scatter(strip.reshape(1, STRIP * size, size), "row", scatter_dimension=1, tiled=True)
        rows = lax.axis_index("row") * share.shape[1] + jnp.arange(share.shape[1], dtype=jnp.int32)
        unit = (rows // size % SPAN == SPAN - 1)[:, None] & ((rows % size)[:, None] == jnp.arange(size)[None, :])
        return share + unit.astype(jnp.float32)[None]

    q2, q3, q1, x_p, far, own = call(
        split_kernel,
        [message(4), message(4), message(4), message(8), full(STRIP + 1), full(STRIP + 1)],
        operands, specs, scratch=[power], aliases={2: 4, 3: 5},
    )
    q2 = swap(q2, "row", 2)
    q3 = swap(q3, "row", 3)
    q1 = swap(q1, "row", 1)
    x_p = swap(x_p, "tile", 2)
    p2, p3, p1, own_p = call(
        after_x_kernel, [message(2)] * 3 + [full(2)], (own, x_p), [VMEM] * 2, scratch=[pltpu.VMEM((8, size, size), jnp.float32), power]
    )
    p2 = swap(p2, "row", 2)
    p3 = swap(p3, "row", 3)
    p1 = swap(p1, "row", 1)
    x_q, own_q = call(after_z_kernel, [message(2), full(2)], (own_p, far, own, q2, q3, q1), [pl.BlockSpec(memory_space=pl.ANY)] + [VMEM] * 5, scratch=[power])
    x_q = swap(x_q, "tile", 2)
    return call(
        last_kernel, jax.ShapeDtypeStruct((1, 4 * size, size), jnp.float32), (own_p, p2, p3, p1, own_q, x_q), [VMEM] * 6
    )


def solution(mesh):
    return jax.shard_map(
        on_device,
        mesh=mesh,
        in_specs=(
            P(("groups", "row", "tile"), None, None, None),
            P(("groups", "row"), None),
            P("groups"),
        ),
        out_specs=P(("groups", "tile"), "row", None),
        check_vma=False,
    )
```

```python
import functools

import jax
import jax.numpy as jnp
from jax import lax
from jax.experimental import pallas as pl
from jax.experimental.pallas import tpu as pltpu
from jax.sharding import PartitionSpec as P

NB = 512
SPAN = 8
STRIP = 2 * SPAN
UNIT = 64
X_FIRST = ((0, 1, 2, 3, 4),)
Z_FIRST = ((5, 6, 7),)

ORDER = (("x", 0), ("z", 0))

VMEM = pl.BlockSpec(memory_space=pltpu.VMEM)
SMEM = pl.BlockSpec(memory_space=pltpu.SMEM)
HBM = pl.BlockSpec(memory_space=pltpu.HBM)
ANY = pl.BlockSpec(memory_space=pl.ANY)
PARAMS = pltpu.CompilerParams(vmem_limit_bytes=32 * 1024 * 1024)


def encode(values):
    top = jnp.max(jnp.abs(values), axis=0, keepdims=True)
    power = jnp.ceil(jnp.log2(jnp.maximum(top, 1e-30)))
    scaled = jnp.round(values * jnp.exp2(15.0 - power))
    codes = jnp.clip(scaled, -32767.0, 32767.0).astype(jnp.int32).astype(jnp.int16)
    return codes, power


def extra_of(count):
    return -(-count // 16) * 16


def pack(units, message_ref, power_ref):
    extra = extra_of(len(units))
    power_ref[...] = jnp.zeros_like(power_ref)
    for at, values in enumerate(units):
        codes, power = encode(values)
        message_ref[at * UNIT : (at + 1) * UNIT, :] = codes
        power_ref[at : at + 1, :] = power
    message_ref[len(units) * UNIT :, :] = power_ref[0:extra, :].astype(jnp.int32).astype(jnp.int16)


def unpacker(message_ref):
    extra = message_ref.shape[0] % UNIT
    first = message_ref.shape[0] - extra
    scales = jnp.exp2(message_ref[first:, :].astype(jnp.int32).astype(jnp.float32) - 15.0)

    def unit(at):
        codes = message_ref[at * UNIT : (at + 1) * UNIT, :].astype(jnp.int32).astype(jnp.float32)
        return codes * scales[at : at + 1, :]

    return unit


def unit_of(sums_ref, owner, unit):
    return sums_ref[4 * owner + unit // 2, unit % 2 * UNIT : (unit % 2 + 1) * UNIT, :]


def plan_of(cols_ref, low_ref, fields_ref, quota):
    here = lax.axis_index("tile")
    cols = cols_ref[...]
    count = cols.shape[1]
    folded = jnp.minimum(cols, NB - 1 - cols)
    near = (folded == low_ref[here]).astype(jnp.int32)
    far = (folded == low_ref[here ^ 2]).astype(jnp.int32)
    hit = near + far
    target = jnp.sum(hit * cols, axis=0, keepdims=True)
    slot = jnp.sum(hit * lax.broadcasted_iota(jnp.int32, cols.shape, 0), axis=0, keepdims=True)
    local = jnp.sum(near, axis=0, keepdims=True)
    wanted = jnp.sum(hit, axis=0, keepdims=True)
    place = cols - target + SPAN - 1
    good = (cols >= 0) & (place >= 0) & (place < SPAN)
    place = jnp.where(good, place + jnp.where(target >= NB // 2, SPAN, 0), STRIP)
    panel = lax.broadcasted_iota(jnp.int32, (1, count), 1)
    device = panel // (4 * quota)
    mate = (device == (here ^ 1)).astype(jnp.int32)
    wanted = (wanted > 0) & ((device == here) | (mate > 0))
    group = jnp.where(wanted, local * 2 + mate, -1)
    members = (lax.broadcasted_iota(jnp.int32, (8, count), 0) == group).astype(jnp.float32)
    before = (
        lax.broadcasted_iota(jnp.int32, (count, count), 0) < lax.broadcasted_iota(jnp.int32, (count, count), 1)
    ).astype(jnp.float32)
    ranks = jnp.dot(members, before, preferred_element_type=jnp.float32)
    rank = jnp.sum(members * ranks, axis=0, keepdims=True).astype(jnp.int32)
    entry = jnp.where(wanted, group * quota + rank, -1)
    chosen = (lax.broadcasted_iota(jnp.int32, (4 * quota, count), 0) == entry).astype(jnp.float32)
    fields_ref[...] = jnp.zeros_like(fields_ref)
    fields_ref[0:1, 0:count] = (panel % (4 * quota)).astype(jnp.float32)
    fields_ref[1:2, 0:count] = slot.astype(jnp.float32)
    fields_ref[2:6, 0:count] = place.astype(jnp.float32)
    table = lax.dot_general(
        chosen, fields_ref[:, 0:count], (((1,), (1,)), ((), ())), preferred_element_type=jnp.float32
    )
    return table.astype(jnp.int32)


def add_products(plan_ref, entry, panels_ref, sums_ref):
    panel = plan_ref[entry, 0]
    column = panels_ref[panel, plan_ref[entry, 1]].T
    size = column.shape[0]
    wide = jnp.concatenate([panels_ref[panel, slot] for slot in range(4)], axis=1)
    made = jnp.dot(column, wide, preferred_element_type=jnp.float32)
    for slot in range(4):
        sums_ref[plan_ref[entry, 2 + slot]] += made[:, slot * size : (slot + 1) * size]


def near_kernel(cols_hbm, low_hbm, blocks_ref, plan_ref, far_ref, own_ref, held, cols_ref, low_ref, fields, table, sems):
    quota = blocks_ref.shape[0] // 4
    cols_copy = pltpu.make_async_copy(cols_hbm, cols_ref, sems.at[0])
    low_copy = pltpu.make_async_copy(low_hbm, low_ref, sems.at[1])
    held_copy = pltpu.make_async_copy(blocks_ref, held, sems.at[2])
    cols_copy.start()
    low_copy.start()
    held_copy.start()
    far_ref[...] = jnp.zeros_like(far_ref)
    own_ref[...] = jnp.zeros_like(own_ref)
    low_copy.wait()
    cols_copy.wait()
    table[:, 0:8] = plan_of(cols_ref, low_ref, fields, quota)
    plan_copy = pltpu.make_async_copy(table, plan_ref, sems.at[3])
    plan_copy.start()
    plan_copy.wait()
    held_copy.wait()
    for at in range(quota):
        add_products(plan_ref, at, held, far_ref)
        add_products(plan_ref, 2 * quota + at, held, own_ref)


def add_mate(plan_ref, mate_ref, far_ref, own_ref):
    quota = mate_ref.shape[0] // 4
    for at in range(quota):
        add_products(plan_ref, quota + at, mate_ref, far_ref)
        add_products(plan_ref, 3 * quota + at, mate_ref, own_ref)


def split_kernel(plan_ref, mate_ref, far_in, own_in, *refs):
    refs, (far_ref, own_ref, power) = list(refs[:-3]), refs[-3:]
    add_mate(plan_ref, mate_ref, far_ref, own_ref)
    here = lax.axis_index("row")
    for units in X_FIRST:
        pack([unit_of(far_ref, owner, unit) for owner in range(4) for unit in units], refs.pop(0), power)
    for units in Z_FIRST:
        for apart in (2, 3, 1):
            owner = here ^ apart
            pack([unit_of(ref, owner, unit) for ref in (far_ref, own_ref) for unit in units], refs.pop(0), power)


def after_x_kernel(units, after_ref, x_ref, own_ref, z2_ref, z3_ref, z1_ref, keep_ref, sums, power):
    here = lax.axis_index("row")
    received = unpacker(x_ref)
    count = len(units)
    for owner in range(4):
        for at, unit in enumerate(units):
            sums[owner * count + at] = unit_of(own_ref, owner, unit) + received(owner * count + at)
    for apart, z_ref in ((2, z2_ref), (3, z3_ref), (1, z1_ref)):
        first = (here ^ apart) * count
        pack([sums[first + at] for at in range(count)], z_ref, power)
    for at in range(count):
        keep_ref[at] = sums[here * count + at]


def after_z_kernel(units, after_ref, z2_ref, z3_ref, z1_ref, far_ref, own_ref, x_ref, keep_ref, power):
    here = lax.axis_index("row")
    received = [unpacker(ref) for ref in (z2_ref, z3_ref, z1_ref)]
    count = len(units)
    totals = []
    for side, sums_ref in enumerate((far_ref, own_ref)):
        for at, unit in enumerate(units):
            total = unit_of(sums_ref, here, unit)
            for part in received:
                total = total + part(side * count + at)
            totals.append(total)
    pack(totals[:count], x_ref, power)
    for at in range(count):
        keep_ref[at] = totals[count + at]


def last_kernel(*refs):
    refs, out_ref = list(refs[:-1]), refs[-1]
    odd = lax.axis_index("row") % 2

    def put(units, keep_ref, parts):
        received = [unpacker(ref) for ref in parts]
        for at, unit in enumerate(units):
            total = keep_ref[at]
            for part in received:
                total = total + part(at)
            if unit >= 6:
                rows = lax.broadcasted_iota(jnp.int32, total.shape, 0) + unit % 2 * UNIT
                columns = lax.broadcasted_iota(jnp.int32, total.shape, 1)
                total = total + jnp.where((rows == columns) & (odd == 1), 1.0, 0.0)
            out_ref[0, unit * UNIT : (unit + 1) * UNIT, :] = total

    for units in Z_FIRST:
        put(units, refs.pop(0), [refs.pop(0)])
    for units in X_FIRST:
        put(units, refs.pop(0), [refs.pop(0) for _ in range(3)])


def full_kernel(plan_ref, mate_ref, far_in, own_in, x_ref, far_ref, own_ref, power):
    add_mate(plan_ref, mate_ref, far_ref, own_ref)
    pack([unit_of(far_ref, owner, unit) for owner in range(4) for unit in range(8)], x_ref, power)


def add_kernel(own_ref, x_ref, sum_ref):
    received = unpacker(x_ref)
    for at in range(4 * 8):
        sum_ref[at * UNIT : (at + 1) * UNIT, :] = unit_of(own_ref, at // 8, at % 8) + received(at)


def call(kernel, outs, operands, specs, out_specs=None, scratch=(), size=1 << 20, aliases=None):
    return pl.pallas_call(
        kernel,
        out_shape=outs,
        in_specs=specs,
        out_specs=jax.tree.map(lambda _: VMEM, outs) if out_specs is None else out_specs,
        scratch_shapes=list(scratch),
        input_output_aliases=aliases or {},
        compiler_params=PARAMS,
        cost_estimate=pl.CostEstimate(flops=0, bytes_accessed=size, transcendentals=0),
    )(*operands)


def on_device(blocks, block_cols, pair_low):
    panels_here, slots, size, _ = blocks.shape
    tiles_count = lax.axis_size("tile")
    rows_count = lax.axis_size("row")
    assert tiles_count == 4 and pair_low.shape[0] == 4 and slots == 4

    def swap(value, axis, apart):
        return lax.ppermute(value, axis, [(i, i ^ apart) for i in range(lax.axis_size(axis))])

    def message(count):
        return jax.ShapeDtypeStruct((count * UNIT + extra_of(count), size), jnp.int16)

    def full(count, rows=size):
        return jax.ShapeDtypeStruct((count, rows, size), jnp.float32)

    power = pltpu.VMEM((32, size), jnp.float32)
    mate = swap(blocks, "tile", 1)
    plan, far, own = call(
        near_kernel,
        [jax.ShapeDtypeStruct((panels_here, 128), jnp.int32), full(STRIP + 1), full(STRIP + 1)],
        tuple(pltpu.with_memory_space_constraint(value, pltpu.HBM) for value in (block_cols.T, pair_low, blocks)),
        [HBM, HBM, HBM],
        [SMEM, VMEM, VMEM],
        [
            pltpu.VMEM(blocks.shape, blocks.dtype),
            pltpu.VMEM(block_cols.shape[::-1], jnp.int32),
            pltpu.SMEM(pair_low.shape, jnp.int32),
            pltpu.VMEM((8, 128), jnp.float32),
            pltpu.VMEM((panels_here, 128), jnp.int32),
            pltpu.SemaphoreType.DMA((4,)),
        ],
        8 << 20,
    )
    operands = (plan, mate, far, own)
    specs = [SMEM, VMEM, VMEM, VMEM]

    if rows_count != 4:
        across, far, own = call(
            full_kernel, [message(4 * 8), far, own], operands, specs, scratch=[power], aliases={2: 1, 3: 2}
        )
        sums = jax.ShapeDtypeStruct((STRIP * size, size), jnp.float32)
        strip = call(add_kernel, sums, (own, swap(across, "tile", 2)), [VMEM, VMEM])
        share = lax.psum_scatter(strip[None], "row", scatter_dimension=1, tiled=True)
        rows = lax.axis_index("row") * share.shape[1] + jnp.arange(share.shape[1], dtype=jnp.int32)
        unit = (rows // size % SPAN == SPAN - 1)[:, None] & ((rows % size)[:, None] == jnp.arange(size)[None, :])
        return share + unit.astype(jnp.float32)[None]

    def over_z(messages):
        return [swap(value, "row", apart) for value, apart in zip(messages, (2, 3, 1))]

    sent = [message(4 * len(units)) for units in X_FIRST]
    for units in Z_FIRST:
        sent += [message(2 * len(units))] * 3
    *made, far, own = call(
        split_kernel, [*sent, full(STRIP + 1), full(STRIP + 1)], operands, specs, scratch=[power],
        aliases={2: len(sent), 3: len(sent) + 1},
    )
    over_x = [swap(made.pop(0), "tile", 2) for units in X_FIRST]
    first_z = [over_z([made.pop(0) for _ in range(3)]) for units in Z_FIRST]
    last = {}
    after = plan

    def run_x(at):
        units = X_FIRST[at]
        count = len(units)
        *onward, keep = call(
            functools.partial(after_x_kernel, units), [message(count)] * 3 + [full(count, UNIT)],
            (after, over_x[at], own), [ANY, VMEM, VMEM],
            scratch=[pltpu.VMEM((4 * count, UNIT, size), jnp.float32), power],
        )
        last["x", at] = [keep, *over_z(onward)]
        return keep

    def run_z(at):
        units = Z_FIRST[at]
        count = len(units)
        onward, keep = call(
            functools.partial(after_z_kernel, units), [message(count), full(count, UNIT)],
            (after, *first_z[at], far, own), [ANY] + [VMEM] * 5, scratch=[power],
        )
        last["z", at] = [keep, swap(onward, "tile", 2)]
        return keep

    for kind, at in ORDER:
        after = (run_x if kind == "x" else run_z)(at)
    parts = [part for at in range(len(Z_FIRST)) for part in last["z", at]]
    parts += [part for at in range(len(X_FIRST)) for part in last["x", at]]
    return call(last_kernel, jax.ShapeDtypeStruct((1, 4 * size, size), jnp.float32), parts, [VMEM] * len(parts))


def solution(mesh):
    return jax.shard_map(
        on_device,
        mesh=mesh,
        in_specs=(
            P(("groups", "row", "tile"), None, None, None),
            P(("groups", "row"), None),
            P("groups"),
        ),
        out_specs=P(("groups", "tile"), "row", None),
        check_vma=False,
    )
```

```python
import functools

import jax
import jax.numpy as jnp
from jax import lax
from jax.experimental import pallas as pl
from jax.experimental.pallas import tpu as pltpu
from jax.sharding import PartitionSpec as P

NB = 512
SPAN = 8
STRIP = 2 * SPAN

X_FIRST = (80, 80, 80, 80)
Z_FIRST = (96, 96)
TILE = 16
X_ROWS = sum(X_FIRST)
Z_ROWS = sum(Z_FIRST)
LENT = len(X_FIRST)
PLAIN = 64

HBM = pl.BlockSpec(memory_space=pltpu.HBM)
ANY = pl.BlockSpec(memory_space=pl.ANY)
VMEM = pl.BlockSpec(memory_space=pltpu.VMEM)
SMEM = pl.BlockSpec(memory_space=pltpu.SMEM)
PARAMS = pltpu.CompilerParams(vmem_limit_bytes=32 * 1024 * 1024)


def spans(groups, first=0):
    return [(first + sum(groups[:at]), rows) for at, rows in enumerate(groups)]


def power_of(*values):
    top = functools.reduce(jnp.maximum, [jnp.max(jnp.abs(v), axis=0, keepdims=True) for v in values])
    return jnp.ceil(jnp.log2(jnp.maximum(top, 1e-30)))


def codes_of(values, power):
    return jnp.clip(jnp.round(values * jnp.exp2(15.0 - power)), -32767.0, 32767.0)


def narrow(codes):
    return codes.astype(jnp.int32).astype(jnp.int16)


def widen(codes):
    return codes.astype(jnp.int32).astype(jnp.float32)


def last_row(rows, size, last, others):
    return jnp.where(lax.broadcasted_iota(jnp.int32, (rows, size), 0) == rows - 1, last, others)


def encode_lent(values):
    power = power_of(values)
    return narrow(last_row(*values.shape, power, codes_of(values, power)))


def decode_lent(codes):
    codes = widen(codes)
    return codes * jnp.exp2(codes[-1:, :] - 15.0)


def part_rows(owner, first, rows, part):
    return pl.ds(pl.multiple_of(owner * part + first, 16), rows)


def lent_row(ref, owner, first, rows, part):
    return ref[pl.ds(pl.multiple_of(owner * part + first + rows - 8, 8), 8), :][7:8, :]


def pack_sides(sides, message_ref, tile_ref):
    count = len(Z_FIRST)
    tile_ref[...] = jnp.zeros_like(tile_ref)
    for side, (groups, lent) in enumerate(sides):
        for at, (values, (first, rows)) in enumerate(zip(groups, spans(Z_FIRST, side * Z_ROWS))):
            power = power_of(values, *lent) if at == 0 else power_of(values)
            message_ref[first : first + rows, :] = narrow(codes_of(values, power))
            row = side * count + at
            tile_ref[row : row + 1, :] = power
            if at == 0:
                for index, value in enumerate(lent):
                    row = len(sides) * count + side * LENT + index
                    tile_ref[row : row + 1, :] = codes_of(value, power)
    message_ref[len(sides) * Z_ROWS :, :] = narrow(tile_ref[...])


def unpack_sides(message_ref, sides):
    count = len(Z_FIRST)
    tile = widen(message_ref[sides * Z_ROWS :, :])
    made = []
    for side in range(sides):
        scales = [jnp.exp2(tile[row : row + 1, :] - 15.0) for row in range(side * count, (side + 1) * count)]
        groups = [
            widen(message_ref[first : first + rows, :]) * scale
            for (first, rows), scale in zip(spans(Z_FIRST, side * Z_ROWS), scales)
        ]
        start = sides * count + side * LENT
        made.append((groups, [tile[row : row + 1, :] * scales[0] for row in range(start, start + LENT)]))
    return made


def plan_of(cols_ref, low_ref, fields_ref, quota):
    here = lax.axis_index("tile")
    cols = cols_ref[...]
    count = cols.shape[1]
    folded = jnp.minimum(cols, NB - 1 - cols)
    near = (folded == low_ref[here]).astype(jnp.int32)
    far = (folded == low_ref[here ^ 2]).astype(jnp.int32)
    hit = near + far
    target = jnp.sum(hit * cols, axis=0, keepdims=True)
    slot = jnp.sum(hit * lax.broadcasted_iota(jnp.int32, cols.shape, 0), axis=0, keepdims=True)
    local = jnp.sum(near, axis=0, keepdims=True)
    wanted = jnp.sum(hit, axis=0, keepdims=True)
    place = cols - target + SPAN - 1
    good = (cols >= 0) & (place >= 0) & (place < SPAN)
    place = jnp.where(good, place + jnp.where(target >= NB // 2, SPAN, 0), STRIP)
    panel = lax.broadcasted_iota(jnp.int32, (1, count), 1)
    device = panel // (4 * quota)
    mate = (device == (here ^ 1)).astype(jnp.int32)
    wanted = (wanted > 0) & ((device == here) | (mate > 0))
    group = jnp.where(wanted, local * 2 + mate, -1)
    members = (lax.broadcasted_iota(jnp.int32, (8, count), 0) == group).astype(jnp.float32)
    before = (
        lax.broadcasted_iota(jnp.int32, (count, count), 0) < lax.broadcasted_iota(jnp.int32, (count, count), 1)
    ).astype(jnp.float32)
    ranks = jnp.dot(members, before, preferred_element_type=jnp.float32)
    rank = jnp.sum(members * ranks, axis=0, keepdims=True).astype(jnp.int32)
    entry = jnp.where(wanted, group * quota + rank, -1)
    chosen = (lax.broadcasted_iota(jnp.int32, (4 * quota, count), 0) == entry).astype(jnp.float32)
    fields_ref[...] = jnp.zeros_like(fields_ref)
    fields_ref[0:1, 0:count] = (panel % (4 * quota)).astype(jnp.float32)
    fields_ref[1:2, 0:count] = slot.astype(jnp.float32)
    fields_ref[2:6, 0:count] = place.astype(jnp.float32)
    table = lax.dot_general(
        chosen, fields_ref[:, 0:count], (((1,), (1,)), ((), ())), preferred_element_type=jnp.float32
    )
    return table.astype(jnp.int32)


def add_products(plan_ref, entry, panels_ref, sums_ref):
    panel = plan_ref[entry, 0]
    column = panels_ref[panel, plan_ref[entry, 1]].T
    size = column.shape[0]
    wide = jnp.concatenate([panels_ref[panel, slot] for slot in range(4)], axis=1)
    made = jnp.dot(column, wide, preferred_element_type=jnp.float32)
    for slot in range(4):
        place = pl.multiple_of(plan_ref[entry, 2 + slot] * size, size)
        sums_ref[pl.ds(place, size), :] += made[:, slot * size : (slot + 1) * size]


def near_kernel(cols_hbm, low_hbm, blocks_ref, plan_ref, far_ref, own_ref, held, cols_ref, low_ref, fields, table, sems):
    quota = blocks_ref.shape[0] // 4
    cols_copy = pltpu.make_async_copy(cols_hbm, cols_ref, sems.at[0])
    low_copy = pltpu.make_async_copy(low_hbm, low_ref, sems.at[1])
    held_copy = pltpu.make_async_copy(blocks_ref, held, sems.at[2])
    cols_copy.start()
    low_copy.start()
    held_copy.start()
    far_ref[...] = jnp.zeros_like(far_ref)
    own_ref[...] = jnp.zeros_like(own_ref)
    low_copy.wait()
    cols_copy.wait()
    table[:, 0:8] = plan_of(cols_ref, low_ref, fields, quota)
    plan_copy = pltpu.make_async_copy(table, plan_ref, sems.at[3])
    plan_copy.start()
    plan_copy.wait()
    held_copy.wait()
    for at in range(quota):
        add_products(plan_ref, at, held, far_ref)
        add_products(plan_ref, 2 * quota + at, held, own_ref)


def add_mate(plan_ref, mate_ref, sums_ref, group):
    quota = mate_ref.shape[0] // 4
    for at in range(quota):
        add_products(plan_ref, group * quota + at, mate_ref, sums_ref)


def sides_of(refs, owner, part):
    return [
        (
            [ref[part_rows(owner, first, rows, part), :] for first, rows in spans(Z_FIRST, X_ROWS)],
            [lent_row(ref, owner, first, rows, part) for first, rows in spans(X_FIRST)],
        )
        for ref in refs
    ]


def pack_z(far_ref, own_ref, z_refs, tile):
    here = lax.axis_index("row")
    part = STRIP * far_ref.shape[1] // 4
    for apart, z_ref in zip((2, 3, 1), z_refs):
        pack_sides(sides_of((far_ref, own_ref), here ^ apart, part), z_ref, tile)


def pack_x(far_ref, x_ref):
    part = STRIP * far_ref.shape[1] // 4
    for owner in range(4):
        for first, rows in spans(X_FIRST):
            start = owner * part + first
            x_ref[owner * X_ROWS + first : owner * X_ROWS + first + rows, :] = encode_lent(far_ref[start : start + rows, :])


def split_kernel(plan_ref, mate_ref, far_in, own_in, x_ref, z2_ref, z3_ref, z1_ref, far_ref, own_ref, tile):
    add_mate(plan_ref, mate_ref, far_ref, 1)
    add_mate(plan_ref, mate_ref, own_ref, 3)
    pack_x(far_ref, x_ref)
    pack_z(far_ref, own_ref, (z2_ref, z3_ref, z1_ref), tile)


def after_x_kernel(x_ref, own_ref, z2_ref, z3_ref, z1_ref, keep_ref):
    here = lax.axis_index("row")
    part = STRIP * own_ref.shape[1] // 4

    def total(owner, first, rows):
        received = decode_lent(x_ref[part_rows(owner, first, rows, X_ROWS), :])
        return own_ref[part_rows(owner, first, rows, part), :] + received

    for apart, z_ref in ((2, z2_ref), (3, z3_ref), (1, z1_ref)):
        for first, rows in spans(X_FIRST):
            z_ref[first : first + rows, :] = encode_lent(total(here ^ apart, first, rows))
    for first, rows in spans(X_FIRST):
        keep_ref[first : first + rows, :] = total(here, first, rows)


def after_z_kernel(after_ref, z2_ref, z3_ref, z1_ref, far_ref, own_ref, x_ref, keep_ref, tile):
    here = lax.axis_index("row")
    part = STRIP * own_ref.shape[1] // 4
    mine = sides_of((far_ref, own_ref), here, part)
    received = [unpack_sides(ref, 2) for ref in (z2_ref, z3_ref, z1_ref)]

    def total(side):
        sides = [mine[side], *[sender[side] for sender in received]]
        return [[sum(values[1:], values[0]) for values in zip(*lists)] for lists in zip(*sides)]

    pack_sides([total(0)], x_ref, tile)
    groups, lent = total(1)
    for values, (first, rows) in zip(groups, spans(Z_FIRST)):
        keep_ref[first : first + rows, :] = values
    for index, value in enumerate(lent):
        keep_ref[Z_ROWS + index : Z_ROWS + index + 1, :] = value


def last_kernel(keep_q, x_ref, keep_p, z2_ref, z3_ref, z1_ref, out_ref):
    odd = lax.axis_index("row") % 2 == 1
    part, size = out_ref.shape[1:]

    def put(values, first, rows):
        if first + rows > part - size:
            row = lax.broadcasted_iota(jnp.int32, (rows, size), 0) + first
            column = lax.broadcasted_iota(jnp.int32, (rows, size), 1) + (part - size)
            values = values + jnp.where((row == column) & odd, 1.0, 0.0)
        out_ref[0, first : first + rows, :] = values

    ((groups, lent),) = unpack_sides(x_ref, 1)
    for values, (first, rows) in zip(groups, spans(Z_FIRST)):
        put(keep_q[first : first + rows, :] + values, X_ROWS + first, rows)
    for index, (first, rows) in enumerate(spans(X_FIRST)):
        values = keep_p[first : first + rows, :]
        for ref in (z2_ref, z3_ref, z1_ref):
            values = values + decode_lent(ref[first : first + rows, :])
        row = Z_ROWS + index
        put(last_row(rows, size, keep_q[row : row + 1, :] + lent[index], values), first, rows)


def all_kernel(plan_ref, mate_ref, far_in, own_in, x_ref, far_ref, own_ref, tile):
    add_mate(plan_ref, mate_ref, far_ref, 1)
    add_mate(plan_ref, mate_ref, own_ref, 3)
    count = tile.shape[0]
    for at in range(count):
        values = far_ref[at * PLAIN : (at + 1) * PLAIN, :]
        power = power_of(values)
        x_ref[at * PLAIN : (at + 1) * PLAIN, :] = narrow(codes_of(values, power))
        tile[at : at + 1, :] = power
    x_ref[count * PLAIN :, :] = narrow(tile[...])


def add_kernel(own_ref, x_ref, sum_ref):
    count = sum_ref.shape[0] // PLAIN
    scales = jnp.exp2(widen(x_ref[count * PLAIN :, :]) - 15.0)
    for at in range(count):
        rows = slice(at * PLAIN, (at + 1) * PLAIN)
        sum_ref[rows, :] = own_ref[rows, :] + widen(x_ref[rows, :]) * scales[at : at + 1, :]


def call(kernel, outs, operands, specs, out_specs=None, scratch=(), size=1 << 20, aliases=None):
    return pl.pallas_call(
        kernel,
        out_shape=outs,
        in_specs=specs,
        out_specs=jax.tree.map(lambda _: VMEM, outs) if out_specs is None else out_specs,
        scratch_shapes=list(scratch),
        input_output_aliases=aliases or {},
        compiler_params=PARAMS,
        cost_estimate=pl.CostEstimate(flops=0, bytes_accessed=size, transcendentals=0),
    )(*operands)


def on_device(blocks, block_cols, pair_low):
    panels_here, slots, size, _ = blocks.shape
    tiles_count = lax.axis_size("tile")
    rows_count = lax.axis_size("row")
    assert tiles_count == 4 and pair_low.shape[0] == 4 and slots == 4
    strip_rows = STRIP * size
    share = strip_rows // 4
    assert X_ROWS + Z_ROWS == share and 2 * (LENT + len(Z_FIRST)) <= TILE

    def swap(value, axis, apart):
        return lax.ppermute(value, axis, [(i, i ^ apart) for i in range(lax.axis_size(axis))])

    def message(rows):
        return jax.ShapeDtypeStruct((rows, size), jnp.int16)

    def full(rows):
        return jax.ShapeDtypeStruct((rows, size), jnp.float32)

    mate = swap(blocks, "tile", 1)
    strip = full(strip_rows + size)
    plan, far, own = call(
        near_kernel,
        [pltpu.SMEM((panels_here, 128), jnp.int32), strip, strip],
        tuple(pltpu.with_memory_space_constraint(value, pltpu.HBM) for value in (block_cols.T, pair_low, blocks)),
        [HBM, HBM, HBM],
        [SMEM, VMEM, VMEM],
        [
            pltpu.VMEM(blocks.shape, blocks.dtype),
            pltpu.VMEM(block_cols.shape[::-1], jnp.int32),
            pltpu.SMEM(pair_low.shape, jnp.int32),
            pltpu.VMEM((8, 128), jnp.float32),
            pltpu.VMEM((panels_here, 128), jnp.int32),
            pltpu.SemaphoreType.DMA((4,)),
        ],
        8 << 20,
    )

    if rows_count != 4:
        groups = strip_rows // PLAIN
        across, far, own = call(
            all_kernel, [message(strip_rows + groups), strip, strip], (plan, mate, far, own), [SMEM] + [VMEM] * 3,
            scratch=[pltpu.VMEM((groups, size), jnp.float32)], aliases={2: 1, 3: 2},
        )
        sums = call(add_kernel, full(strip_rows), (own, swap(across, "tile", 2)), [VMEM, VMEM])
        part = lax.psum_scatter(sums[None], "row", scatter_dimension=1, tiled=True)
        rows = lax.axis_index("row") * part.shape[1] + jnp.arange(part.shape[1], dtype=jnp.int32)
        unit = (rows // size % SPAN == SPAN - 1)[:, None] & ((rows % size)[:, None] == jnp.arange(size)[None, :])
        return part + unit.astype(jnp.float32)[None]

    def over_z(messages):
        return [swap(value, "row", apart) for value, apart in zip(messages, (2, 3, 1))]

    tile = pltpu.VMEM((TILE, size), jnp.float32)
    z_sent = [message(2 * Z_ROWS + TILE)] * 3
    p_x, *q_z, far, own = call(
        split_kernel, [message(4 * X_ROWS), *z_sent, strip, strip], (plan, mate, far, own), [SMEM] + [VMEM] * 3,
        scratch=[tile], aliases={2: 4, 3: 5},
    )
    p_x = swap(p_x, "tile", 2)
    q_z = over_z(q_z)
    *p_z, p_keep = call(after_x_kernel, [message(X_ROWS)] * 3 + [full(X_ROWS)], (p_x, own), [VMEM, VMEM])
    p_z = over_z(p_z)
    q_x, q_keep = call(
        after_z_kernel, [message(Z_ROWS + TILE), full(Z_ROWS + 8)],
        (p_keep, *q_z, far, own), [ANY] + [VMEM] * 5, scratch=[tile],
    )
    q_x = swap(q_x, "tile", 2)
    out = jax.ShapeDtypeStruct((1, share, size), jnp.float32)
    return call(last_kernel, out, (q_keep, q_x, p_keep, *p_z), [VMEM] * 6)


def solution(mesh):
    return jax.shard_map(
        on_device,
        mesh=mesh,
        in_specs=(
            P(("groups", "row", "tile"), None, None, None),
            P(("groups", "row"), None),
            P("groups"),
        ),
        out_specs=P(("groups", "tile"), "row", None),
        check_vma=False,
    )
```

```python
import functools

import jax
import jax.numpy as jnp
from jax import lax
from jax.experimental import pallas as pl
from jax.experimental.pallas import tpu as pltpu
from jax.sharding import PartitionSpec as P

NB = 512
SPAN = 8
STRIP = 2 * SPAN

SPLIT = (240, 240, 512, 240)
BLOCK = 128
ORDER = (2, 3, 1)
X_FIRST = ((2,), (0, 3, 1))
TAIL_CUT = 2

HBM = pl.BlockSpec(memory_space=pltpu.HBM)
ANY = pl.BlockSpec(memory_space=pl.ANY)
VMEM = pl.BlockSpec(memory_space=pltpu.VMEM)
SMEM = pl.BlockSpec(memory_space=pltpu.SMEM)
PARAMS = pltpu.CompilerParams(vmem_limit_bytes=32 * 1024 * 1024)


def cut(first, last, count):
    edges = [first + (last - first) * at // count // 16 * 16 for at in range(count)] + [last]
    return list(zip(edges, edges[1:]))


def groups_of(first, last):
    return [(low, high - low) for low, high in cut(first, last, -(-(last - first) // BLOCK))]


def early(part):
    made = [[(apart, groups_of(0, SPLIT[apart])) for apart in held if SPLIT[apart] > 0] for held in X_FIRST]
    return [message for message in made if message]


def z_first(part):
    made = []
    for apart in ORDER:
        if SPLIT[apart] < part:
            made.append((apart, groups_of(SPLIT[apart], part)))
    return made


def tail(part):
    return [groups_of(*rows) for rows in cut(SPLIT[0], part, TAIL_CUT)]


def message_rows(groups):
    return sum(rows for _, rows in groups) + -(-len(groups) // 16) * 16


def power_of(values):
    top = jnp.max(jnp.abs(values), axis=0, keepdims=True)
    return jnp.ceil(jnp.log2(jnp.maximum(top, 1e-30)))


def widen(codes):
    return codes.astype(jnp.int32).astype(jnp.float32)


def pack(groups, message_ref, tile_ref):
    first = 0
    tile_ref[...] = jnp.zeros_like(tile_ref)
    for at, values in enumerate(groups):
        power = power_of(values)
        codes = jnp.clip(jnp.round(values * jnp.exp2(15.0 - power)), -32767.0, 32767.0)
        message_ref[first : first + values.shape[0], :] = codes.astype(jnp.int32).astype(jnp.int16)
        tile_ref[at : at + 1, :] = power
        first += values.shape[0]
    extra = message_ref.shape[0] - first
    message_ref[first:, :] = tile_ref[0:extra, :].astype(jnp.int32).astype(jnp.int16)


def unpack(message_ref, groups):
    total = sum(rows for _, rows in groups)
    scales = jnp.exp2(widen(message_ref[total:, :]) - 15.0)
    made = []
    first = 0
    for at, (_, rows) in enumerate(groups):
        made.append(widen(message_ref[first : first + rows, :]) * scales[at : at + 1, :])
        first += rows
    return made


def part_rows(owner, first, rows, part):
    return pl.ds(pl.multiple_of(owner * part + first, 16), rows)


def plan_of(cols_ref, low_ref, fields_ref, quota):
    here = lax.axis_index("tile")
    cols = cols_ref[...]
    count = cols.shape[1]
    folded = jnp.minimum(cols, NB - 1 - cols)
    near = (folded == low_ref[here]).astype(jnp.int32)
    far = (folded == low_ref[here ^ 2]).astype(jnp.int32)
    hit = near + far
    target = jnp.sum(hit * cols, axis=0, keepdims=True)
    slot = jnp.sum(hit * lax.broadcasted_iota(jnp.int32, cols.shape, 0), axis=0, keepdims=True)
    local = jnp.sum(near, axis=0, keepdims=True)
    wanted = jnp.sum(hit, axis=0, keepdims=True)
    place = cols - target + SPAN - 1
    good = (cols >= 0) & (place >= 0) & (place < SPAN)
    place = jnp.where(good, place + jnp.where(target >= NB // 2, SPAN, 0), STRIP)
    panel = lax.broadcasted_iota(jnp.int32, (1, count), 1)
    device = panel // (4 * quota)
    mate = (device == (here ^ 1)).astype(jnp.int32)
    wanted = (wanted > 0) & ((device == here) | (mate > 0))
    group = jnp.where(wanted, local * 2 + mate, -1)
    members = (lax.broadcasted_iota(jnp.int32, (8, count), 0) == group).astype(jnp.float32)
    before = (
        lax.broadcasted_iota(jnp.int32, (count, count), 0) < lax.broadcasted_iota(jnp.int32, (count, count), 1)
    ).astype(jnp.float32)
    ranks = jnp.dot(members, before, preferred_element_type=jnp.float32)
    rank = jnp.sum(members * ranks, axis=0, keepdims=True).astype(jnp.int32)
    entry = jnp.where(wanted, group * quota + rank, -1)
    chosen = (lax.broadcasted_iota(jnp.int32, (4 * quota, count), 0) == entry).astype(jnp.float32)
    fields_ref[...] = jnp.zeros_like(fields_ref)
    fields_ref[0:1, 0:count] = (panel % (4 * quota)).astype(jnp.float32)
    fields_ref[1:2, 0:count] = slot.astype(jnp.float32)
    fields_ref[2:6, 0:count] = place.astype(jnp.float32)
    table = lax.dot_general(
        chosen, fields_ref[:, 0:count], (((1,), (1,)), ((), ())), preferred_element_type=jnp.float32
    )
    return table.astype(jnp.int32)


def add_products(plan_ref, entry, panels_ref, sums_ref):
    panel = plan_ref[entry, 0]
    column = panels_ref[panel, plan_ref[entry, 1]].T
    size = column.shape[0]
    wide = jnp.concatenate([panels_ref[panel, slot] for slot in range(4)], axis=1)
    made = jnp.dot(column, wide, preferred_element_type=jnp.float32)
    for slot in range(4):
        place = pl.multiple_of(plan_ref[entry, 2 + slot] * size, size)
        sums_ref[pl.ds(place, size), :] += made[:, slot * size : (slot + 1) * size]


def near_kernel(cols_hbm, low_hbm, blocks_ref, plan_ref, far_ref, own_ref, held, cols_ref, low_ref, fields, table, sems):
    quota = blocks_ref.shape[0] // 4
    cols_copy = pltpu.make_async_copy(cols_hbm, cols_ref, sems.at[0])
    low_copy = pltpu.make_async_copy(low_hbm, low_ref, sems.at[1])
    held_copy = pltpu.make_async_copy(blocks_ref, held, sems.at[2])
    cols_copy.start()
    low_copy.start()
    held_copy.start()
    far_ref[...] = jnp.zeros_like(far_ref)
    own_ref[...] = jnp.zeros_like(own_ref)
    low_copy.wait()
    cols_copy.wait()
    table[:, 0:8] = plan_of(cols_ref, low_ref, fields, quota)
    plan_copy = pltpu.make_async_copy(table, plan_ref, sems.at[3])
    plan_copy.start()
    plan_copy.wait()
    held_copy.wait()
    for at in range(quota):
        add_products(plan_ref, at, held, far_ref)
        add_products(plan_ref, 2 * quota + at, held, own_ref)


def add_mate(plan_ref, mate_ref, sums_ref, group):
    quota = mate_ref.shape[0] // 4
    for at in range(quota):
        add_products(plan_ref, group * quota + at, mate_ref, sums_ref)


def split_kernel(plan_ref, mate_ref, far_in, own_in, *refs):
    *refs, far_ref, own_ref, tile = refs
    add_mate(plan_ref, mate_ref, far_ref, 1)
    add_mate(plan_ref, mate_ref, own_ref, 3)
    here = lax.axis_index("row")
    part = STRIP * far_ref.shape[1] // 4
    for held in early(part):
        groups = [far_ref[part_rows(here ^ apart, *group, part), :] for apart, groups in held for group in groups]
        pack(groups, refs.pop(0), tile)
    for apart, groups in z_first(part):
        groups = [ref[part_rows(here ^ apart, *group, part), :] for ref in (far_ref, own_ref) for group in groups]
        pack(groups, refs.pop(0), tile)


def after_x_kernel(held, after_ref, x_ref, own_ref, *refs):
    *refs, tile = refs
    here = lax.axis_index("row")
    part = STRIP * own_ref.shape[1] // 4
    received = unpack(x_ref, [group for _, groups in held for group in groups])
    for apart, groups in held:
        totals = [own_ref[part_rows(here ^ apart, *group, part), :] + received.pop(0) for group in groups]
        if apart == 0:
            refs[0][...] = jnp.concatenate(totals)
        else:
            pack(totals, refs[0], tile)
        refs = refs[1:]


def after_z_kernel(after_ref, far_ref, own_ref, *refs):
    z_refs, x_refs = refs[: len(refs) - TAIL_CUT - 3], refs[len(refs) - TAIL_CUT - 3 : -3]
    keep_ref, far_sum, tile = refs[-3:]
    here = lax.axis_index("row")
    part = STRIP * own_ref.shape[1] // 4
    first = SPLIT[0]
    for sums_ref, total_ref in ((far_ref, far_sum), (own_ref, keep_ref)):
        total_ref[...] = sums_ref[part_rows(here, first, part - first, part), :]
    for (apart, groups), z_ref in zip(z_first(part), z_refs):
        received = unpack(z_ref, 2 * groups)
        for total_ref in (far_sum, keep_ref):
            for low, rows in groups:
                total_ref[low - first : low - first + rows, :] += received.pop(0)
    for groups, x_ref in zip(tail(part), x_refs):
        pack([far_sum[low - first : low - first + rows, :] for low, rows in groups], x_ref, tile)


def last_kernel(keep_q, keep_p, *refs):
    x_refs, z_refs, out_ref = refs[:TAIL_CUT], refs[TAIL_CUT:-1], refs[-1]
    part, size = out_ref.shape[1:]
    first = SPLIT[0]
    if first > 0:
        out_ref[0, 0:first, :] = keep_p[...]
    for groups, x_ref in zip(tail(part), x_refs):
        for (low, rows), values in zip(groups, unpack(x_ref, groups)):
            out_ref[0, low : low + rows, :] = keep_q[low - first : low - first + rows, :] + values
    came = dict(pair for held in early(part) for pair in held)
    for apart, z_ref in zip([apart for apart in ORDER if apart in came], z_refs):
        for (low, rows), values in zip(came[apart], unpack(z_ref, came[apart])):
            out_ref[0, low : low + rows, :] += values
    row = lax.broadcasted_iota(jnp.int32, (size, size), 0)
    column = lax.broadcasted_iota(jnp.int32, (size, size), 1)
    odd = lax.axis_index("row") % 2 == 1
    out_ref[0, part - size :, :] += jnp.where((row == column) & odd, 1.0, 0.0)


def all_kernel(plan_ref, mate_ref, far_in, own_in, x_ref, far_ref, own_ref, tile):
    add_mate(plan_ref, mate_ref, far_ref, 1)
    add_mate(plan_ref, mate_ref, own_ref, 3)
    size = far_ref.shape[1]
    pack([far_ref[low : low + rows, :] for low, rows in groups_of(0, STRIP * size)], x_ref, tile)


def add_kernel(own_ref, x_ref, sum_ref):
    groups = groups_of(0, sum_ref.shape[0])
    for (low, rows), values in zip(groups, unpack(x_ref, groups)):
        sum_ref[low : low + rows, :] = own_ref[low : low + rows, :] + values


def call(kernel, outs, operands, specs, out_specs=None, scratch=(), size=1 << 20, aliases=None):
    return pl.pallas_call(
        kernel,
        out_shape=outs,
        in_specs=specs,
        out_specs=jax.tree.map(lambda _: VMEM, outs) if out_specs is None else out_specs,
        scratch_shapes=list(scratch),
        input_output_aliases=aliases or {},
        compiler_params=PARAMS,
        cost_estimate=pl.CostEstimate(flops=0, bytes_accessed=size, transcendentals=0),
    )(*operands)


def on_device(blocks, block_cols, pair_low):
    panels_here, slots, size, _ = blocks.shape
    tiles_count = lax.axis_size("tile")
    rows_count = lax.axis_size("row")
    assert tiles_count == 4 and pair_low.shape[0] == 4 and slots == 4
    strip_rows = STRIP * size
    share = strip_rows // 4
    assert SPLIT[0] == SPLIT[1] <= min(SPLIT[2:]) and max(SPLIT) <= share

    def swap(value, axis, apart):
        return lax.ppermute(value, axis, [(i, i ^ apart) for i in range(lax.axis_size(axis))])

    def message(groups):
        return jax.ShapeDtypeStruct((message_rows(groups), size), jnp.int16)

    def full(rows):
        return jax.ShapeDtypeStruct((rows, size), jnp.float32)

    mate = swap(blocks, "tile", 1)
    strip = full(strip_rows + size)
    plan, far, own = call(
        near_kernel,
        [pltpu.SMEM((panels_here, 128), jnp.int32), strip, strip],
        tuple(pltpu.with_memory_space_constraint(value, pltpu.HBM) for value in (block_cols.T, pair_low, blocks)),
        [HBM, HBM, HBM],
        [SMEM, VMEM, VMEM],
        [
            pltpu.VMEM(blocks.shape, blocks.dtype),
            pltpu.VMEM(block_cols.shape[::-1], jnp.int32),
            pltpu.SMEM(pair_low.shape, jnp.int32),
            pltpu.VMEM((8, 128), jnp.float32),
            pltpu.VMEM((panels_here, 128), jnp.int32),
            pltpu.SemaphoreType.DMA((4,)),
        ],
        8 << 20,
    )

    tile = pltpu.VMEM((32, size), jnp.float32)

    if rows_count != 4:
        across, far, own = call(
            all_kernel, [message(groups_of(0, strip_rows)), strip, strip], (plan, mate, far, own), [SMEM] + [VMEM] * 3,
            scratch=[tile], aliases={2: 1, 3: 2},
        )
        sums = call(add_kernel, full(strip_rows), (own, swap(across, "tile", 2)), [VMEM, VMEM])
        part = lax.psum_scatter(sums[None], "row", scatter_dimension=1, tiled=True)
        rows = lax.axis_index("row") * part.shape[1] + jnp.arange(part.shape[1], dtype=jnp.int32)
        unit = (rows // size % SPAN == SPAN - 1)[:, None] & ((rows % size)[:, None] == jnp.arange(size)[None, :])
        return part + unit.astype(jnp.float32)[None]

    x_sent, z_sent = early(share), z_first(share)
    x_groups = [[group for _, groups in held for group in groups] for held in x_sent]
    *made, far, own = call(
        split_kernel,
        [*[message(groups) for groups in x_groups], *[message(2 * groups) for _, groups in z_sent], strip, strip],
        (plan, mate, far, own), [SMEM] + [VMEM] * 3, scratch=[tile],
        aliases={2: len(x_sent) + len(z_sent), 3: len(x_sent) + len(z_sent) + 1},
    )
    over_x = [swap(made.pop(0), "tile", 2) for _ in x_sent]
    q_z = [swap(made.pop(0), "row", apart) for apart, _ in z_sent]
    after, second = plan, {}
    for held, value in zip(x_sent, over_x):
        results = [full(SPLIT[0]) if apart == 0 else message(groups) for apart, groups in held]
        results = call(
            functools.partial(after_x_kernel, held), results, (after, value, own), [ANY, VMEM, VMEM], scratch=[tile]
        )
        after = results[0]
        for (apart, _), value in zip(held, results):
            second[apart] = value if apart == 0 else swap(value, "row", apart)
    p_keep = second.get(0, plan)
    p_z = [second[apart] for apart in ORDER if apart in second]
    rest = share - SPLIT[0]
    *q_x, q_keep = call(
        after_z_kernel, [*[message(groups) for groups in tail(share)], full(rest)], (after, far, own, *q_z),
        [ANY] + [VMEM] * (2 + len(q_z)), scratch=[pltpu.VMEM((rest, size), jnp.float32), tile],
    )
    q_x = [swap(value, "tile", 2) for value in q_x]
    out = jax.ShapeDtypeStruct((1, share, size), jnp.float32)
    return call(last_kernel, out, (q_keep, p_keep, *q_x, *p_z), [VMEM, VMEM if 0 in second else ANY] + [VMEM] * (len(q_x) + len(p_z)))


def solution(mesh):
    return jax.shard_map(
        on_device,
        mesh=mesh,
        in_specs=(
            P(("groups", "row", "tile"), None, None, None),
            P(("groups", "row"), None),
            P("groups"),
        ),
        out_specs=P(("groups", "tile"), "row", None),
        check_vma=False,
    )
```

```python
import functools

import jax
import jax.numpy as jnp
from jax import lax
from jax.experimental import pallas as pl
from jax.experimental.pallas import tpu as pltpu
from jax.sharding import PartitionSpec as P

NB = 512
SPAN = 8
STRIP = 2 * SPAN

SPLIT = (240, 240, 512, 240)
BLOCK = 128
ORDER = (2, 3, 1)
X_FIRST = ((2, 0), (1, 3))
TAIL_CUT = 2
TAIL_ROWS = 208

HBM = pl.BlockSpec(memory_space=pltpu.HBM)
ANY = pl.BlockSpec(memory_space=pl.ANY)
VMEM = pl.BlockSpec(memory_space=pltpu.VMEM)
SMEM = pl.BlockSpec(memory_space=pltpu.SMEM)
PARAMS = pltpu.CompilerParams(vmem_limit_bytes=32 * 1024 * 1024)


def cut(first, last, count):
    edges = [first + (last - first) * at // count // 16 * 16 for at in range(count)] + [last]
    return list(zip(edges, edges[1:]))


def groups_of(first, last):
    return [(low, high - low) for low, high in cut(first, last, -(-(last - first) // BLOCK))]


def early(part):
    made = [[(apart, groups_of(0, SPLIT[apart])) for apart in held if SPLIT[apart] > 0] for held in X_FIRST]
    return [message for message in made if message]


def z_first(part):
    made = []
    for apart in ORDER:
        if SPLIT[apart] < part:
            made.append((apart, groups_of(SPLIT[apart], part)))
    return made


def tail(part):
    middle = SPLIT[0] + TAIL_ROWS
    return [groups_of(SPLIT[0], middle), groups_of(middle, part)]


def message_rows(groups):
    return sum(rows for _, rows in groups) + -(-len(groups) // 16) * 16


def power_of(values):
    top = jnp.max(jnp.abs(values), axis=0, keepdims=True)
    return jnp.ceil(jnp.log2(jnp.maximum(top, 1e-30)))


def widen(codes):
    return codes.astype(jnp.int32).astype(jnp.float32)


def pack(groups, message_ref, tile_ref):
    first = 0
    tile_ref[...] = jnp.zeros_like(tile_ref)
    for at, values in enumerate(groups):
        power = power_of(values)
        codes = jnp.clip(jnp.round(values * jnp.exp2(15.0 - power)), -32767.0, 32767.0)
        message_ref[first : first + values.shape[0], :] = codes.astype(jnp.int32).astype(jnp.int16)
        tile_ref[at : at + 1, :] = power
        first += values.shape[0]
    extra = message_ref.shape[0] - first
    message_ref[first:, :] = tile_ref[0:extra, :].astype(jnp.int32).astype(jnp.int16)


def unpack(message_ref, groups):
    total = sum(rows for _, rows in groups)
    scales = jnp.exp2(widen(message_ref[total:, :]) - 15.0)
    made = []
    first = 0
    for at, (_, rows) in enumerate(groups):
        made.append(widen(message_ref[first : first + rows, :]) * scales[at : at + 1, :])
        first += rows
    return made


def part_rows(owner, first, rows, part):
    return pl.ds(pl.multiple_of(owner * part + first, 16), rows)


def plan_of(cols_ref, low_ref, fields_ref, quota):
    here = lax.axis_index("tile")
    cols = cols_ref[...]
    count = cols.shape[1]
    folded = jnp.minimum(cols, NB - 1 - cols)
    near = (folded == low_ref[here]).astype(jnp.int32)
    far = (folded == low_ref[here ^ 2]).astype(jnp.int32)
    hit = near + far
    target = jnp.sum(hit * cols, axis=0, keepdims=True)
    slot = jnp.sum(hit * lax.broadcasted_iota(jnp.int32, cols.shape, 0), axis=0, keepdims=True)
    local = jnp.sum(near, axis=0, keepdims=True)
    wanted = jnp.sum(hit, axis=0, keepdims=True)
    place = cols - target + SPAN - 1
    good = (cols >= 0) & (place >= 0) & (place < SPAN)
    place = jnp.where(good, place + jnp.where(target >= NB // 2, SPAN, 0), STRIP)
    panel = lax.broadcasted_iota(jnp.int32, (1, count), 1)
    device = panel // (4 * quota)
    mate = (device == (here ^ 1)).astype(jnp.int32)
    wanted = (wanted > 0) & ((device == here) | (mate > 0))
    group = jnp.where(wanted, local * 2 + mate, -1)
    members = (lax.broadcasted_iota(jnp.int32, (8, count), 0) == group).astype(jnp.float32)
    before = (
        lax.broadcasted_iota(jnp.int32, (count, count), 0) < lax.broadcasted_iota(jnp.int32, (count, count), 1)
    ).astype(jnp.float32)
    ranks = jnp.dot(members, before, preferred_element_type=jnp.float32)
    rank = jnp.sum(members * ranks, axis=0, keepdims=True).astype(jnp.int32)
    entry = jnp.where(wanted, group * quota + rank, -1)
    chosen = (lax.broadcasted_iota(jnp.int32, (4 * quota, count), 0) == entry).astype(jnp.float32)
    fields_ref[...] = jnp.zeros_like(fields_ref)
    fields_ref[0:1, 0:count] = (panel % (4 * quota)).astype(jnp.float32)
    fields_ref[1:2, 0:count] = slot.astype(jnp.float32)
    fields_ref[2:6, 0:count] = place.astype(jnp.float32)
    table = lax.dot_general(
        chosen, fields_ref[:, 0:count], (((1,), (1,)), ((), ())), preferred_element_type=jnp.float32
    )
    return table.astype(jnp.int32)


def add_products(plan_ref, entry, panels_ref, sums_ref):
    panel = plan_ref[entry, 0]
    column = panels_ref[panel, plan_ref[entry, 1]].T
    size = column.shape[0]
    wide = jnp.concatenate([panels_ref[panel, slot] for slot in range(4)], axis=1)
    made = jnp.dot(column, wide, preferred_element_type=jnp.float32)
    for slot in range(4):
        place = pl.multiple_of(plan_ref[entry, 2 + slot] * size, size)
        sums_ref[pl.ds(place, size), :] += made[:, slot * size : (slot + 1) * size]


def near_kernel(cols_hbm, low_hbm, blocks_ref, plan_ref, far_ref, own_ref, held, cols_ref, low_ref, fields, table, sems):
    quota = blocks_ref.shape[0] // 4
    cols_copy = pltpu.make_async_copy(cols_hbm, cols_ref, sems.at[0])
    low_copy = pltpu.make_async_copy(low_hbm, low_ref, sems.at[1])
    held_copy = pltpu.make_async_copy(blocks_ref, held, sems.at[2])
    cols_copy.start()
    low_copy.start()
    held_copy.start()
    far_ref[...] = jnp.zeros_like(far_ref)
    own_ref[...] = jnp.zeros_like(own_ref)
    low_copy.wait()
    cols_copy.wait()
    table[:, 0:8] = plan_of(cols_ref, low_ref, fields, quota)
    plan_copy = pltpu.make_async_copy(table, plan_ref, sems.at[3])
    plan_copy.start()
    plan_copy.wait()
    held_copy.wait()
    for at in range(quota):
        add_products(plan_ref, at, held, far_ref)
        add_products(plan_ref, 2 * quota + at, held, own_ref)


def add_mate(plan_ref, mate_ref, sums_ref, group):
    quota = mate_ref.shape[0] // 4
    for at in range(quota):
        add_products(plan_ref, group * quota + at, mate_ref, sums_ref)


def split_kernel(plan_ref, mate_ref, far_in, own_in, *refs):
    *refs, far_ref, own_ref, tile = refs
    add_mate(plan_ref, mate_ref, far_ref, 1)
    add_mate(plan_ref, mate_ref, own_ref, 3)
    here = lax.axis_index("row")
    part = STRIP * far_ref.shape[1] // 4
    for held in early(part):
        groups = [far_ref[part_rows(here ^ apart, *group, part), :] for apart, groups in held for group in groups]
        pack(groups, refs.pop(0), tile)
    for apart, groups in z_first(part):
        groups = [ref[part_rows(here ^ apart, *group, part), :] for ref in (far_ref, own_ref) for group in groups]
        pack(groups, refs.pop(0), tile)


def after_x_kernel(held, after_ref, x_ref, own_ref, *refs):
    *refs, tile = refs
    here = lax.axis_index("row")
    part = STRIP * own_ref.shape[1] // 4
    received = unpack(x_ref, [group for _, groups in held for group in groups])
    for apart, groups in held:
        totals = [own_ref[part_rows(here ^ apart, *group, part), :] + received.pop(0) for group in groups]
        if apart == 0:
            refs[0][...] = jnp.concatenate(totals)
        else:
            pack(totals, refs[0], tile)
        refs = refs[1:]


def after_z_kernel(after_ref, far_ref, own_ref, *refs):
    z_refs, x_refs = refs[: len(refs) - TAIL_CUT - 3], refs[len(refs) - TAIL_CUT - 3 : -3]
    keep_ref, far_sum, tile = refs[-3:]
    here = lax.axis_index("row")
    part = STRIP * own_ref.shape[1] // 4
    first = SPLIT[0]
    for sums_ref, total_ref in ((far_ref, far_sum), (own_ref, keep_ref)):
        total_ref[...] = sums_ref[part_rows(here, first, part - first, part), :]
    for (apart, groups), z_ref in zip(z_first(part), z_refs):
        received = unpack(z_ref, 2 * groups)
        for total_ref in (far_sum, keep_ref):
            for low, rows in groups:
                total_ref[low - first : low - first + rows, :] += received.pop(0)
    for groups, x_ref in zip(tail(part), x_refs):
        pack([far_sum[low - first : low - first + rows, :] for low, rows in groups], x_ref, tile)


def last_kernel(keep_q, keep_p, *refs):
    x_refs, z_refs, out_ref = refs[:TAIL_CUT], refs[TAIL_CUT:-1], refs[-1]
    part, size = out_ref.shape[1:]
    first = SPLIT[0]
    if first > 0:
        out_ref[0, 0:first, :] = keep_p[...]
    for groups, x_ref in zip(tail(part), x_refs):
        for (low, rows), values in zip(groups, unpack(x_ref, groups)):
            out_ref[0, low : low + rows, :] = keep_q[low - first : low - first + rows, :] + values
    came = dict(pair for held in early(part) for pair in held)
    for apart, z_ref in zip([apart for apart in ORDER if apart in came], z_refs):
        for (low, rows), values in zip(came[apart], unpack(z_ref, came[apart])):
            out_ref[0, low : low + rows, :] += values
    row = lax.broadcasted_iota(jnp.int32, (size, size), 0)
    column = lax.broadcasted_iota(jnp.int32, (size, size), 1)
    odd = lax.axis_index("row") % 2 == 1
    out_ref[0, part - size :, :] += jnp.where((row == column) & odd, 1.0, 0.0)


def all_kernel(plan_ref, mate_ref, far_in, own_in, x_ref, far_ref, own_ref, tile):
    add_mate(plan_ref, mate_ref, far_ref, 1)
    add_mate(plan_ref, mate_ref, own_ref, 3)
    size = far_ref.shape[1]
    pack([far_ref[low : low + rows, :] for low, rows in groups_of(0, STRIP * size)], x_ref, tile)


def add_kernel(own_ref, x_ref, sum_ref):
    groups = groups_of(0, sum_ref.shape[0])
    for (low, rows), values in zip(groups, unpack(x_ref, groups)):
        sum_ref[low : low + rows, :] = own_ref[low : low + rows, :] + values


def call(kernel, outs, operands, specs, out_specs=None, scratch=(), size=1 << 20, aliases=None):
    return pl.pallas_call(
        kernel,
        out_shape=outs,
        in_specs=specs,
        out_specs=jax.tree.map(lambda _: VMEM, outs) if out_specs is None else out_specs,
        scratch_shapes=list(scratch),
        input_output_aliases=aliases or {},
        compiler_params=PARAMS,
        cost_estimate=pl.CostEstimate(flops=0, bytes_accessed=size, transcendentals=0),
    )(*operands)


def on_device(blocks, block_cols, pair_low):
    panels_here, slots, size, _ = blocks.shape
    tiles_count = lax.axis_size("tile")
    rows_count = lax.axis_size("row")
    assert tiles_count == 4 and pair_low.shape[0] == 4 and slots == 4
    strip_rows = STRIP * size
    share = strip_rows // 4
    assert SPLIT[0] == SPLIT[1] <= min(SPLIT[2:]) and max(SPLIT) <= share

    def swap(value, axis, apart):
        return lax.ppermute(value, axis, [(i, i ^ apart) for i in range(lax.axis_size(axis))])

    def message(groups):
        return jax.ShapeDtypeStruct((message_rows(groups), size), jnp.int16)

    def full(rows):
        return jax.ShapeDtypeStruct((rows, size), jnp.float32)

    mate = swap(blocks, "tile", 1)
    strip = full(strip_rows + size)
    plan, far, own = call(
        near_kernel,
        [pltpu.SMEM((panels_here, 128), jnp.int32), strip, strip],
        tuple(pltpu.with_memory_space_constraint(value, pltpu.HBM) for value in (block_cols.T, pair_low, blocks)),
        [HBM, HBM, HBM],
        [SMEM, VMEM, VMEM],
        [
            pltpu.VMEM(blocks.shape, blocks.dtype),
            pltpu.VMEM(block_cols.shape[::-1], jnp.int32),
            pltpu.SMEM(pair_low.shape, jnp.int32),
            pltpu.VMEM((8, 128), jnp.float32),
            pltpu.VMEM((panels_here, 128), jnp.int32),
            pltpu.SemaphoreType.DMA((4,)),
        ],
        8 << 20,
    )

    tile = pltpu.VMEM((32, size), jnp.float32)

    if rows_count != 4:
        across, far, own = call(
            all_kernel, [message(groups_of(0, strip_rows)), strip, strip], (plan, mate, far, own), [SMEM] + [VMEM] * 3,
            scratch=[tile], aliases={2: 1, 3: 2},
        )
        sums = call(add_kernel, full(strip_rows), (own, swap(across, "tile", 2)), [VMEM, VMEM])
        part = lax.psum_scatter(sums[None], "row", scatter_dimension=1, tiled=True)
        rows = lax.axis_index("row") * part.shape[1] + jnp.arange(part.shape[1], dtype=jnp.int32)
        unit = (rows // size % SPAN == SPAN - 1)[:, None] & ((rows % size)[:, None] == jnp.arange(size)[None, :])
        return part + unit.astype(jnp.float32)[None]

    x_sent, z_sent = early(share), z_first(share)
    x_groups = [[group for _, groups in held for group in groups] for held in x_sent]
    *made, far, own = call(
        split_kernel,
        [*[message(groups) for groups in x_groups], *[message(2 * groups) for _, groups in z_sent], strip, strip],
        (plan, mate, far, own), [SMEM] + [VMEM] * 3, scratch=[tile],
        aliases={2: len(x_sent) + len(z_sent), 3: len(x_sent) + len(z_sent) + 1},
    )
    over_x = [swap(made.pop(0), "tile", 2) for _ in x_sent]
    q_z = [swap(made.pop(0), "row", apart) for apart, _ in z_sent]
    after, second = plan, {}
    for held, value in zip(x_sent, over_x):
        results = [full(SPLIT[0]) if apart == 0 else message(groups) for apart, groups in held]
        results = call(
            functools.partial(after_x_kernel, held), results, (after, value, own), [ANY, VMEM, VMEM], scratch=[tile]
        )
        after = results[0]
        for (apart, _), value in zip(held, results):
            second[apart] = value if apart == 0 else swap(value, "row", apart)
    p_keep = second.get(0, plan)
    p_z = [second[apart] for apart in ORDER if apart in second]
    rest = share - SPLIT[0]
    *q_x, q_keep = call(
        after_z_kernel, [*[message(groups) for groups in tail(share)], full(rest)], (after, far, own, *q_z),
        [ANY] + [VMEM] * (2 + len(q_z)), scratch=[pltpu.VMEM((rest, size), jnp.float32), tile],
    )
    q_x = [swap(value, "tile", 2) for value in q_x]
    out = jax.ShapeDtypeStruct((1, share, size), jnp.float32)
    return call(last_kernel, out, (q_keep, p_keep, *q_x, *p_z), [VMEM, VMEM if 0 in second else ANY] + [VMEM] * (len(q_x) + len(p_z)))


def solution(mesh):
    return jax.shard_map(
        on_device,
        mesh=mesh,
        in_specs=(
            P(("groups", "row", "tile"), None, None, None),
            P(("groups", "row"), None),
            P("groups"),
        ),
        out_specs=P(("groups", "tile"), "row", None),
        check_vma=False,
    )
```

```python
import functools

import jax
import jax.numpy as jnp
from jax import lax
from jax.experimental import pallas as pl
from jax.experimental.pallas import tpu as pltpu
from jax.sharding import PartitionSpec as P

NB = 512
SPAN = 8
STRIP = 2 * SPAN

SPLIT = (240, 240, 512, 240)
BLOCK = 128
ORDER = (2, 3, 1)
X_FIRST = ((2, 0), (1, 3))
TAIL_CUT = 2
TAIL_ROWS = 208

HBM = pl.BlockSpec(memory_space=pltpu.HBM)
ANY = pl.BlockSpec(memory_space=pl.ANY)
VMEM = pl.BlockSpec(memory_space=pltpu.VMEM)
SMEM = pl.BlockSpec(memory_space=pltpu.SMEM)
PARAMS = pltpu.CompilerParams(vmem_limit_bytes=32 * 1024 * 1024)


def cut(first, last, count):
    edges = [first + (last - first) * at // count // 16 * 16 for at in range(count)] + [last]
    return list(zip(edges, edges[1:]))


def groups_of(first, last):
    return [(low, high - low) for low, high in cut(first, last, -(-(last - first) // BLOCK))]


def early(part):
    made = [[(apart, groups_of(0, SPLIT[apart])) for apart in held if SPLIT[apart] > 0] for held in X_FIRST]
    return [message for message in made if message]


def z_first(part):
    made = []
    for apart in ORDER:
        if SPLIT[apart] < part:
            made.append((apart, groups_of(SPLIT[apart], part)))
    return made


def tail(part):
    middle = SPLIT[0] + TAIL_ROWS
    return [groups_of(SPLIT[0], middle), groups_of(middle, part)]


def message_rows(groups):
    return sum(rows for _, rows in groups) + -(-len(groups) // 16) * 16


def power_of(values):
    top = jnp.max(jnp.abs(values), axis=0, keepdims=True)
    return jnp.ceil(jnp.log2(jnp.maximum(top, 1e-30)))


def widen(codes):
    return codes.astype(jnp.int32).astype(jnp.float32)


def pack(groups, message_ref, tile_ref):
    first = 0
    tile_ref[...] = jnp.zeros_like(tile_ref)
    for at, values in enumerate(groups):
        power = power_of(values)
        codes = jnp.clip(jnp.round(values * jnp.exp2(15.0 - power)), -32767.0, 32767.0)
        message_ref[first : first + values.shape[0], :] = codes.astype(jnp.int32).astype(jnp.int16)
        tile_ref[at : at + 1, :] = power
        first += values.shape[0]
    extra = message_ref.shape[0] - first
    message_ref[first:, :] = tile_ref[0:extra, :].astype(jnp.int32).astype(jnp.int16)


def unpack(message_ref, groups):
    total = sum(rows for _, rows in groups)
    scales = jnp.exp2(widen(message_ref[total:, :]) - 15.0)
    made = []
    first = 0
    for at, (_, rows) in enumerate(groups):
        made.append(widen(message_ref[first : first + rows, :]) * scales[at : at + 1, :])
        first += rows
    return made


def part_rows(owner, first, rows, part):
    return pl.ds(pl.multiple_of(owner * part + first, 16), rows)


def plan_of(cols_ref, low_ref, fields_ref, quota):
    here = lax.axis_index("tile")
    cols = cols_ref[...]
    count = cols.shape[1]
    folded = jnp.minimum(cols, NB - 1 - cols)
    near = (folded == low_ref[here]).astype(jnp.int32)
    far = (folded == low_ref[here ^ 2]).astype(jnp.int32)
    hit = near + far
    target = jnp.sum(hit * cols, axis=0, keepdims=True)
    slot = jnp.sum(hit * lax.broadcasted_iota(jnp.int32, cols.shape, 0), axis=0, keepdims=True)
    local = jnp.sum(near, axis=0, keepdims=True)
    wanted = jnp.sum(hit, axis=0, keepdims=True)
    place = cols - target + SPAN - 1
    good = (cols >= 0) & (place >= 0) & (place < SPAN)
    place = jnp.where(good, place + jnp.where(target >= NB // 2, SPAN, 0), STRIP)
    panel = lax.broadcasted_iota(jnp.int32, (1, count), 1)
    device = panel // (4 * quota)
    mate = (device == (here ^ 1)).astype(jnp.int32)
    wanted = (wanted > 0) & ((device == here) | (mate > 0))
    group = jnp.where(wanted, local * 2 + mate, -1)
    members = (lax.broadcasted_iota(jnp.int32, (8, count), 0) == group).astype(jnp.float32)
    before = (
        lax.broadcasted_iota(jnp.int32, (count, count), 0) < lax.broadcasted_iota(jnp.int32, (count, count), 1)
    ).astype(jnp.float32)
    ranks = jnp.dot(members, before, preferred_element_type=jnp.float32)
    rank = jnp.sum(members * ranks, axis=0, keepdims=True).astype(jnp.int32)
    entry = jnp.where(wanted, group * quota + rank, -1)
    chosen = (lax.broadcasted_iota(jnp.int32, (4 * quota, count), 0) == entry).astype(jnp.float32)
    fields_ref[...] = jnp.zeros_like(fields_ref)
    fields_ref[0:1, 0:count] = (panel % (4 * quota)).astype(jnp.float32)
    fields_ref[1:2, 0:count] = slot.astype(jnp.float32)
    fields_ref[2:6, 0:count] = place.astype(jnp.float32)
    table = lax.dot_general(
        chosen, fields_ref[:, 0:count], (((1,), (1,)), ((), ())), preferred_element_type=jnp.float32
    )
    return table.astype(jnp.int32)


def add_products(plan_ref, entry, panels_ref, sums_ref):
    panel = plan_ref[entry, 0]
    column = panels_ref[panel, plan_ref[entry, 1]].T
    size = column.shape[0]
    wide = jnp.concatenate([panels_ref[panel, slot] for slot in range(4)], axis=1)
    made = jnp.dot(column, wide, preferred_element_type=jnp.float32)
    for slot in range(4):
        place = pl.multiple_of(plan_ref[entry, 2 + slot] * size, size)
        sums_ref[pl.ds(place, size), :] += made[:, slot * size : (slot + 1) * size]


def near_kernel(cols_hbm, low_hbm, blocks_ref, plan_ref, far_ref, own_ref, held, cols_ref, low_ref, fields, table, sems):
    quota = blocks_ref.shape[0] // 4
    cols_copy = pltpu.make_async_copy(cols_hbm, cols_ref, sems.at[0])
    low_copy = pltpu.make_async_copy(low_hbm, low_ref, sems.at[1])
    held_copy = pltpu.make_async_copy(blocks_ref, held, sems.at[2])
    cols_copy.start()
    low_copy.start()
    held_copy.start()
    far_ref[...] = jnp.zeros_like(far_ref)
    own_ref[...] = jnp.zeros_like(own_ref)
    low_copy.wait()
    cols_copy.wait()
    table[:, 0:8] = plan_of(cols_ref, low_ref, fields, quota)
    plan_copy = pltpu.make_async_copy(table, plan_ref, sems.at[3])
    plan_copy.start()
    plan_copy.wait()
    held_copy.wait()
    for at in range(quota):
        add_products(plan_ref, at, held, far_ref)
        add_products(plan_ref, 2 * quota + at, held, own_ref)


def add_mate(plan_ref, mate_ref, sums_ref, group):
    quota = mate_ref.shape[0] // 4
    for at in range(quota):
        add_products(plan_ref, group * quota + at, mate_ref, sums_ref)


def pack_x(held, here, part, far_ref, x_ref, tile):
    groups = [far_ref[part_rows(here ^ apart, *group, part), :] for apart, groups in held for group in groups]
    pack(groups, x_ref, tile)


def sums_kernel(plan_ref, mate_ref, far_in, x_ref, far_ref, tile):
    add_mate(plan_ref, mate_ref, far_ref, 1)
    part = STRIP * far_ref.shape[1] // 4
    pack_x(early(part)[0], lax.axis_index("row"), part, far_ref, x_ref, tile)


def split_kernel(plan_ref, mate_ref, far_ref, own_in, *refs):
    *refs, own_ref, tile = refs
    add_mate(plan_ref, mate_ref, own_ref, 3)
    here = lax.axis_index("row")
    part = STRIP * far_ref.shape[1] // 4
    for held in early(part)[1:]:
        pack_x(held, here, part, far_ref, refs.pop(0), tile)
    for apart, groups in z_first(part):
        groups = [ref[part_rows(here ^ apart, *group, part), :] for ref in (far_ref, own_ref) for group in groups]
        pack(groups, refs.pop(0), tile)


def after_x_kernel(held, after_ref, x_ref, own_ref, *refs):
    *refs, tile = refs
    here = lax.axis_index("row")
    part = STRIP * own_ref.shape[1] // 4
    received = unpack(x_ref, [group for _, groups in held for group in groups])
    for apart, groups in held:
        totals = [own_ref[part_rows(here ^ apart, *group, part), :] + received.pop(0) for group in groups]
        if apart == 0:
            refs[0][...] = jnp.concatenate(totals)
        else:
            pack(totals, refs[0], tile)
        refs = refs[1:]


def after_z_kernel(after_ref, far_ref, own_ref, *refs):
    z_refs, x_refs = refs[: len(refs) - TAIL_CUT - 3], refs[len(refs) - TAIL_CUT - 3 : -3]
    keep_ref, far_sum, tile = refs[-3:]
    here = lax.axis_index("row")
    part = STRIP * own_ref.shape[1] // 4
    first = SPLIT[0]
    for sums_ref, total_ref in ((far_ref, far_sum), (own_ref, keep_ref)):
        total_ref[...] = sums_ref[part_rows(here, first, part - first, part), :]
    for (apart, groups), z_ref in zip(z_first(part), z_refs):
        received = unpack(z_ref, 2 * groups)
        for total_ref in (far_sum, keep_ref):
            for low, rows in groups:
                total_ref[low - first : low - first + rows, :] += received.pop(0)
    for groups, x_ref in zip(tail(part), x_refs):
        pack([far_sum[low - first : low - first + rows, :] for low, rows in groups], x_ref, tile)


def last_kernel(keep_q, keep_p, *refs):
    x_refs, z_refs, out_ref = refs[:TAIL_CUT], refs[TAIL_CUT:-1], refs[-1]
    part, size = out_ref.shape[1:]
    first = SPLIT[0]
    if first > 0:
        out_ref[0, 0:first, :] = keep_p[...]
    for groups, x_ref in zip(tail(part), x_refs):
        for (low, rows), values in zip(groups, unpack(x_ref, groups)):
            out_ref[0, low : low + rows, :] = keep_q[low - first : low - first + rows, :] + values
    came = dict(pair for held in early(part) for pair in held)
    for apart, z_ref in zip([apart for apart in ORDER if apart in came], z_refs):
        for (low, rows), values in zip(came[apart], unpack(z_ref, came[apart])):
            out_ref[0, low : low + rows, :] += values
    row = lax.broadcasted_iota(jnp.int32, (size, size), 0)
    column = lax.broadcasted_iota(jnp.int32, (size, size), 1)
    odd = lax.axis_index("row") % 2 == 1
    out_ref[0, part - size :, :] += jnp.where((row == column) & odd, 1.0, 0.0)


def all_kernel(plan_ref, mate_ref, far_in, own_in, x_ref, far_ref, own_ref, tile):
    add_mate(plan_ref, mate_ref, far_ref, 1)
    add_mate(plan_ref, mate_ref, own_ref, 3)
    size = far_ref.shape[1]
    pack([far_ref[low : low + rows, :] for low, rows in groups_of(0, STRIP * size)], x_ref, tile)


def add_kernel(own_ref, x_ref, sum_ref):
    groups = groups_of(0, sum_ref.shape[0])
    for (low, rows), values in zip(groups, unpack(x_ref, groups)):
        sum_ref[low : low + rows, :] = own_ref[low : low + rows, :] + values


def call(kernel, outs, operands, specs, out_specs=None, scratch=(), size=1 << 20, aliases=None):
    return pl.pallas_call(
        kernel,
        out_shape=outs,
        in_specs=specs,
        out_specs=jax.tree.map(lambda _: VMEM, outs) if out_specs is None else out_specs,
        scratch_shapes=list(scratch),
        input_output_aliases=aliases or {},
        compiler_params=PARAMS,
        cost_estimate=pl.CostEstimate(flops=0, bytes_accessed=size, transcendentals=0),
    )(*operands)


def on_device(blocks, block_cols, pair_low):
    panels_here, slots, size, _ = blocks.shape
    tiles_count = lax.axis_size("tile")
    rows_count = lax.axis_size("row")
    assert tiles_count == 4 and pair_low.shape[0] == 4 and slots == 4
    strip_rows = STRIP * size
    share = strip_rows // 4
    assert SPLIT[0] == SPLIT[1] <= min(SPLIT[2:]) and max(SPLIT) <= share

    def swap(value, axis, apart):
        return lax.ppermute(value, axis, [(i, i ^ apart) for i in range(lax.axis_size(axis))])

    def message(groups):
        return jax.ShapeDtypeStruct((message_rows(groups), size), jnp.int16)

    def full(rows):
        return jax.ShapeDtypeStruct((rows, size), jnp.float32)

    mate = swap(blocks, "tile", 1)
    strip = full(strip_rows + size)
    plan, far, own = call(
        near_kernel,
        [pltpu.SMEM((panels_here, 128), jnp.int32), strip, strip],
        tuple(pltpu.with_memory_space_constraint(value, pltpu.HBM) for value in (block_cols.T, pair_low, blocks)),
        [HBM, HBM, HBM],
        [SMEM, VMEM, VMEM],
        [
            pltpu.VMEM(blocks.shape, blocks.dtype),
            pltpu.VMEM(block_cols.shape[::-1], jnp.int32),
            pltpu.SMEM(pair_low.shape, jnp.int32),
            pltpu.VMEM((8, 128), jnp.float32),
            pltpu.VMEM((panels_here, 128), jnp.int32),
            pltpu.SemaphoreType.DMA((4,)),
        ],
        8 << 20,
    )

    tile = pltpu.VMEM((32, size), jnp.float32)

    if rows_count != 4:
        across, far, own = call(
            all_kernel, [message(groups_of(0, strip_rows)), strip, strip], (plan, mate, far, own), [SMEM] + [VMEM] * 3,
            scratch=[tile], aliases={2: 1, 3: 2},
        )
        sums = call(add_kernel, full(strip_rows), (own, swap(across, "tile", 2)), [VMEM, VMEM])
        part = lax.psum_scatter(sums[None], "row", scatter_dimension=1, tiled=True)
        rows = lax.axis_index("row") * part.shape[1] + jnp.arange(part.shape[1], dtype=jnp.int32)
        unit = (rows // size % SPAN == SPAN - 1)[:, None] & ((rows % size)[:, None] == jnp.arange(size)[None, :])
        return part + unit.astype(jnp.float32)[None]

    x_sent, z_sent = early(share), z_first(share)
    x_groups = [[group for _, groups in held for group in groups] for held in x_sent]
    first, far = call(
        sums_kernel, [message(x_groups[0]), strip], (plan, mate, far), [SMEM] + [VMEM] * 2, scratch=[tile], aliases={2: 1}
    )
    rest_sent = [*[message(groups) for groups in x_groups[1:]], *[message(2 * groups) for _, groups in z_sent]]
    *made, own = call(
        split_kernel, [*rest_sent, strip], (plan, mate, far, own), [SMEM] + [VMEM] * 3, scratch=[tile],
        aliases={3: len(rest_sent)},
    )
    made = [first, *made]
    over_x = [swap(made.pop(0), "tile", 2) for _ in x_sent]
    q_z = [swap(made.pop(0), "row", apart) for apart, _ in z_sent]
    after, second = plan, {}
    for held, value in zip(x_sent, over_x):
        results = [full(SPLIT[0]) if apart == 0 else message(groups) for apart, groups in held]
        results = call(
            functools.partial(after_x_kernel, held), results, (after, value, own), [ANY, VMEM, VMEM], scratch=[tile]
        )
        after = results[0]
        for (apart, _), value in zip(held, results):
            second[apart] = value if apart == 0 else swap(value, "row", apart)
    p_keep = second.get(0, plan)
    p_z = [second[apart] for apart in ORDER if apart in second]
    rest = share - SPLIT[0]
    *q_x, q_keep = call(
        after_z_kernel, [*[message(groups) for groups in tail(share)], full(rest)], (after, far, own, *q_z),
        [ANY] + [VMEM] * (2 + len(q_z)), scratch=[pltpu.VMEM((rest, size), jnp.float32), tile],
    )
    q_x = [swap(value, "tile", 2) for value in q_x]
    out = jax.ShapeDtypeStruct((1, share, size), jnp.float32)
    return call(last_kernel, out, (q_keep, p_keep, *q_x, *p_z), [VMEM, VMEM if 0 in second else ANY] + [VMEM] * (len(q_x) + len(p_z)))


def solution(mesh):
    return jax.shard_map(
        on_device,
        mesh=mesh,
        in_specs=(
            P(("groups", "row", "tile"), None, None, None),
            P(("groups", "row"), None),
            P("groups"),
        ),
        out_specs=P(("groups", "tile"), "row", None),
        check_vma=False,
    )
```

```python
import functools

import jax
import jax.numpy as jnp
from jax import lax
from jax.experimental import pallas as pl
from jax.experimental.pallas import tpu as pltpu
from jax.sharding import PartitionSpec as P

NB = 512
SPAN = 8
STRIP = 2 * SPAN

SPLIT = (240, 240, 512, 240)
BLOCK = 128
ORDER = (2, 3, 1)
X_FIRST = ((2, 0), (1, 3))
TAIL_CUT = 2
TAIL_ROWS = 208

HBM = pl.BlockSpec(memory_space=pltpu.HBM)
ANY = pl.BlockSpec(memory_space=pl.ANY)
VMEM = pl.BlockSpec(memory_space=pltpu.VMEM)
SMEM = pl.BlockSpec(memory_space=pltpu.SMEM)
PARAMS = pltpu.CompilerParams(vmem_limit_bytes=32 * 1024 * 1024)


def cut(first, last, count):
    edges = [first + (last - first) * at // count // 16 * 16 for at in range(count)] + [last]
    return list(zip(edges, edges[1:]))


def groups_of(first, last):
    return [(low, high - low) for low, high in cut(first, last, -(-(last - first) // BLOCK))]


def early(part):
    made = [[(apart, groups_of(0, SPLIT[apart])) for apart in held if SPLIT[apart] > 0] for held in X_FIRST]
    return [message for message in made if message]


def z_first(part):
    made = []
    for apart in ORDER:
        if SPLIT[apart] < part:
            made.append((apart, groups_of(SPLIT[apart], part)))
    return made


def tail(part):
    middle = SPLIT[0] + TAIL_ROWS
    return [groups_of(SPLIT[0], middle), groups_of(middle, part)]


def message_rows(groups):
    return sum(rows for _, rows in groups) + -(-len(groups) // 16) * 16


def power_of(values):
    top = jnp.max(jnp.abs(values), axis=0, keepdims=True)
    return jnp.ceil(jnp.log2(jnp.maximum(top, 1e-30)))


def widen(codes):
    return codes.astype(jnp.int32).astype(jnp.float32)


def pack(groups, message_ref, tile_ref):
    first = 0
    tile_ref[...] = jnp.zeros_like(tile_ref)
    for at, values in enumerate(groups):
        power = power_of(values)
        codes = jnp.clip(jnp.round(values * jnp.exp2(15.0 - power)), -32767.0, 32767.0)
        message_ref[first : first + values.shape[0], :] = codes.astype(jnp.int32).astype(jnp.int16)
        tile_ref[at : at + 1, :] = power
        first += values.shape[0]
    extra = message_ref.shape[0] - first
    message_ref[first:, :] = tile_ref[0:extra, :].astype(jnp.int32).astype(jnp.int16)


def unpack(message_ref, groups):
    total = sum(rows for _, rows in groups)
    scales = jnp.exp2(widen(message_ref[total:, :]) - 15.0)
    made = []
    first = 0
    for at, (_, rows) in enumerate(groups):
        made.append(widen(message_ref[first : first + rows, :]) * scales[at : at + 1, :])
        first += rows
    return made


def part_rows(owner, first, rows, part):
    return pl.ds(pl.multiple_of(owner * part + first, 16), rows)


def plan_of(cols_ref, low_ref, fields_ref, quota):
    here = lax.axis_index("tile")
    cols = cols_ref[...]
    count = cols.shape[1]
    folded = jnp.minimum(cols, NB - 1 - cols)
    near = (folded == low_ref[here]).astype(jnp.int32)
    far = (folded == low_ref[here ^ 2]).astype(jnp.int32)
    hit = near + far
    target = jnp.sum(hit * cols, axis=0, keepdims=True)
    slot = jnp.sum(hit * lax.broadcasted_iota(jnp.int32, cols.shape, 0), axis=0, keepdims=True)
    local = jnp.sum(near, axis=0, keepdims=True)
    wanted = jnp.sum(hit, axis=0, keepdims=True)
    place = cols - target + SPAN - 1
    good = (cols >= 0) & (place >= 0) & (place < SPAN)
    place = jnp.where(good, place + jnp.where(target >= NB // 2, SPAN, 0), STRIP)
    panel = lax.broadcasted_iota(jnp.int32, (1, count), 1)
    device = panel // (4 * quota)
    mate = (device == (here ^ 1)).astype(jnp.int32)
    wanted = (wanted > 0) & ((device == here) | (mate > 0))
    group = jnp.where(wanted, local * 2 + mate, -1)
    members = (lax.broadcasted_iota(jnp.int32, (8, count), 0) == group).astype(jnp.float32)
    before = (
        lax.broadcasted_iota(jnp.int32, (count, count), 0) < lax.broadcasted_iota(jnp.int32, (count, count), 1)
    ).astype(jnp.float32)
    ranks = jnp.dot(members, before, preferred_element_type=jnp.float32)
    rank = jnp.sum(members * ranks, axis=0, keepdims=True).astype(jnp.int32)
    entry = jnp.where(wanted, group * quota + rank, -1)
    chosen = (lax.broadcasted_iota(jnp.int32, (4 * quota, count), 0) == entry).astype(jnp.float32)
    fields_ref[...] = jnp.zeros_like(fields_ref)
    fields_ref[0:1, 0:count] = (panel % (4 * quota)).astype(jnp.float32)
    fields_ref[1:2, 0:count] = slot.astype(jnp.float32)
    fields_ref[2:6, 0:count] = place.astype(jnp.float32)
    table = lax.dot_general(
        chosen, fields_ref[:, 0:count], (((1,), (1,)), ((), ())), preferred_element_type=jnp.float32
    )
    return table.astype(jnp.int32)


def add_products(plan_ref, entry, panels_ref, sums_ref):
    panel = plan_ref[entry, 0]
    column = panels_ref[panel, plan_ref[entry, 1]].T
    size = column.shape[0]
    wide = jnp.concatenate([panels_ref[panel, slot] for slot in range(4)], axis=1)
    made = jnp.dot(column, wide, preferred_element_type=jnp.float32)
    for slot in range(4):
        place = pl.multiple_of(plan_ref[entry, 2 + slot] * size, size)
        sums_ref[pl.ds(place, size), :] += made[:, slot * size : (slot + 1) * size]


def near_kernel(cols_hbm, low_hbm, blocks_ref, plan_ref, far_ref, own_ref, held, cols_ref, low_ref, fields, table, sems):
    quota = blocks_ref.shape[0] // 4
    cols_copy = pltpu.make_async_copy(cols_hbm, cols_ref, sems.at[0])
    low_copy = pltpu.make_async_copy(low_hbm, low_ref, sems.at[1])
    held_copy = pltpu.make_async_copy(blocks_ref, held, sems.at[2])
    cols_copy.start()
    low_copy.start()
    held_copy.start()
    far_ref[...] = jnp.zeros_like(far_ref)
    own_ref[...] = jnp.zeros_like(own_ref)
    low_copy.wait()
    cols_copy.wait()
    table[:, 0:8] = plan_of(cols_ref, low_ref, fields, quota)
    plan_copy = pltpu.make_async_copy(table, plan_ref, sems.at[3])
    plan_copy.start()
    plan_copy.wait()
    held_copy.wait()
    for at in range(quota):
        add_products(plan_ref, at, held, far_ref)
        add_products(plan_ref, 2 * quota + at, held, own_ref)


def add_mate(plan_ref, mate_ref, far_ref, own_ref):
    quota = mate_ref.shape[0] // 4
    for at in range(quota):
        add_products(plan_ref, quota + at, mate_ref, far_ref)
        add_products(plan_ref, 3 * quota + at, mate_ref, own_ref)


def split_kernel(plan_ref, mate_ref, far_in, own_in, *refs):
    *refs, far_ref, own_ref, tile = refs
    add_mate(plan_ref, mate_ref, far_ref, own_ref)
    here = lax.axis_index("row")
    part = STRIP * far_ref.shape[1] // 4
    for held in early(part):
        groups = [far_ref[part_rows(here ^ apart, *group, part), :] for apart, groups in held for group in groups]
        pack(groups, refs.pop(0), tile)
    for apart, groups in z_first(part):
        groups = [ref[part_rows(here ^ apart, *group, part), :] for ref in (far_ref, own_ref) for group in groups]
        pack(groups, refs.pop(0), tile)


def after_x_kernel(held, after_ref, x_ref, own_ref, *refs):
    *refs, tile = refs
    here = lax.axis_index("row")
    part = STRIP * own_ref.shape[1] // 4
    received = unpack(x_ref, [group for _, groups in held for group in groups])
    for apart, groups in held:
        totals = [own_ref[part_rows(here ^ apart, *group, part), :] + received.pop(0) for group in groups]
        if apart == 0:
            refs[0][...] = jnp.concatenate(totals)
        else:
            pack(totals, refs[0], tile)
        refs = refs[1:]


def after_z_kernel(after_ref, far_ref, own_ref, *refs):
    z_refs, x_refs = refs[: len(refs) - TAIL_CUT - 3], refs[len(refs) - TAIL_CUT - 3 : -3]
    keep_ref, far_sum, tile = refs[-3:]
    here = lax.axis_index("row")
    part = STRIP * own_ref.shape[1] // 4
    first = SPLIT[0]
    for sums_ref, total_ref in ((far_ref, far_sum), (own_ref, keep_ref)):
        total_ref[...] = sums_ref[part_rows(here, first, part - first, part), :]
    for (apart, groups), z_ref in zip(z_first(part), z_refs):
        received = unpack(z_ref, 2 * groups)
        for total_ref in (far_sum, keep_ref):
            for low, rows in groups:
                total_ref[low - first : low - first + rows, :] += received.pop(0)
    for groups, x_ref in zip(tail(part), x_refs):
        pack([far_sum[low - first : low - first + rows, :] for low, rows in groups], x_ref, tile)


def last_kernel(keep_q, keep_p, *refs):
    x_refs, z_refs, out_ref = refs[:TAIL_CUT], refs[TAIL_CUT:-1], refs[-1]
    part, size = out_ref.shape[1:]
    first = SPLIT[0]
    if first > 0:
        out_ref[0, 0:first, :] = keep_p[...]
    for groups, x_ref in zip(tail(part), x_refs):
        for (low, rows), values in zip(groups, unpack(x_ref, groups)):
            out_ref[0, low : low + rows, :] = keep_q[low - first : low - first + rows, :] + values
    came = dict(pair for held in early(part) for pair in held)
    for apart, z_ref in zip([apart for apart in ORDER if apart in came], z_refs):
        for (low, rows), values in zip(came[apart], unpack(z_ref, came[apart])):
            out_ref[0, low : low + rows, :] += values
    row = lax.broadcasted_iota(jnp.int32, (size, size), 0)
    column = lax.broadcasted_iota(jnp.int32, (size, size), 1)
    odd = lax.axis_index("row") % 2 == 1
    out_ref[0, part - size :, :] += jnp.where((row == column) & odd, 1.0, 0.0)


def all_kernel(plan_ref, mate_ref, far_in, own_in, x_ref, far_ref, own_ref, tile):
    add_mate(plan_ref, mate_ref, far_ref, own_ref)
    size = far_ref.shape[1]
    pack([far_ref[low : low + rows, :] for low, rows in groups_of(0, STRIP * size)], x_ref, tile)


def add_kernel(own_ref, x_ref, sum_ref):
    groups = groups_of(0, sum_ref.shape[0])
    for (low, rows), values in zip(groups, unpack(x_ref, groups)):
        sum_ref[low : low + rows, :] = own_ref[low : low + rows, :] + values


def call(kernel, outs, operands, specs, out_specs=None, scratch=(), size=1 << 20, aliases=None):
    return pl.pallas_call(
        kernel,
        out_shape=outs,
        in_specs=specs,
        out_specs=jax.tree.map(lambda _: VMEM, outs) if out_specs is None else out_specs,
        scratch_shapes=list(scratch),
        input_output_aliases=aliases or {},
        compiler_params=PARAMS,
        cost_estimate=pl.CostEstimate(flops=0, bytes_accessed=size, transcendentals=0),
    )(*operands)


def on_device(blocks, block_cols, pair_low):
    panels_here, slots, size, _ = blocks.shape
    tiles_count = lax.axis_size("tile")
    rows_count = lax.axis_size("row")
    assert tiles_count == 4 and pair_low.shape[0] == 4 and slots == 4
    strip_rows = STRIP * size
    share = strip_rows // 4
    assert SPLIT[0] == SPLIT[1] <= min(SPLIT[2:]) and max(SPLIT) <= share

    def swap(value, axis, apart):
        return lax.ppermute(value, axis, [(i, i ^ apart) for i in range(lax.axis_size(axis))])

    def message(groups):
        return jax.ShapeDtypeStruct((message_rows(groups), size), jnp.int16)

    def full(rows):
        return jax.ShapeDtypeStruct((rows, size), jnp.float32)

    mate = swap(blocks, "tile", 1)
    strip = full(strip_rows + size)
    plan, far, own = call(
        near_kernel,
        [pltpu.SMEM((panels_here, 128), jnp.int32), strip, strip],
        tuple(pltpu.with_memory_space_constraint(value, pltpu.HBM) for value in (block_cols.T, pair_low, blocks)),
        [HBM, HBM, HBM],
        [SMEM, VMEM, VMEM],
        [
            pltpu.VMEM(blocks.shape, blocks.dtype),
            pltpu.VMEM(block_cols.shape[::-1], jnp.int32),
            pltpu.SMEM(pair_low.shape, jnp.int32),
            pltpu.VMEM((8, 128), jnp.float32),
            pltpu.VMEM((panels_here, 128), jnp.int32),
            pltpu.SemaphoreType.DMA((4,)),
        ],
        8 << 20,
    )

    tile = pltpu.VMEM((32, size), jnp.float32)

    if rows_count != 4:
        across, far, own = call(
            all_kernel, [message(groups_of(0, strip_rows)), strip, strip], (plan, mate, far, own), [SMEM] + [VMEM] * 3,
            scratch=[tile], aliases={2: 1, 3: 2},
        )
        sums = call(add_kernel, full(strip_rows), (own, swap(across, "tile", 2)), [VMEM, VMEM])
        part = lax.psum_scatter(sums[None], "row", scatter_dimension=1, tiled=True)
        rows = lax.axis_index("row") * part.shape[1] + jnp.arange(part.shape[1], dtype=jnp.int32)
        unit = (rows // size % SPAN == SPAN - 1)[:, None] & ((rows % size)[:, None] == jnp.arange(size)[None, :])
        return part + unit.astype(jnp.float32)[None]

    x_sent, z_sent = early(share), z_first(share)
    x_groups = [[group for _, groups in held for group in groups] for held in x_sent]
    *made, far, own = call(
        split_kernel,
        [*[message(groups) for groups in x_groups], *[message(2 * groups) for _, groups in z_sent], strip, strip],
        (plan, mate, far, own), [SMEM] + [VMEM] * 3, scratch=[tile],
        aliases={2: len(x_sent) + len(z_sent), 3: len(x_sent) + len(z_sent) + 1},
    )
    over_x = [swap(made.pop(0), "tile", 2) for _ in x_sent]
    q_z = [swap(made.pop(0), "row", apart) for apart, _ in z_sent]
    after, second = plan, {}
    for held, value in zip(x_sent, over_x):
        results = [full(SPLIT[0]) if apart == 0 else message(groups) for apart, groups in held]
        results = call(
            functools.partial(after_x_kernel, held), results, (after, value, own), [ANY, VMEM, VMEM], scratch=[tile]
        )
        after = results[0]
        for (apart, _), value in zip(held, results):
            second[apart] = value if apart == 0 else swap(value, "row", apart)
    p_keep = second.get(0, plan)
    p_z = [second[apart] for apart in ORDER if apart in second]
    rest = share - SPLIT[0]
    *q_x, q_keep = call(
        after_z_kernel, [*[message(groups) for groups in tail(share)], full(rest)], (after, far, own, *q_z),
        [ANY] + [VMEM] * (2 + len(q_z)), scratch=[pltpu.VMEM((rest, size), jnp.float32), tile],
    )
    q_x = [swap(value, "tile", 2) for value in q_x]
    out = jax.ShapeDtypeStruct((1, share, size), jnp.float32)
    return call(last_kernel, out, (q_keep, p_keep, *q_x, *p_z), [VMEM, VMEM if 0 in second else ANY] + [VMEM] * (len(q_x) + len(p_z)))


def solution(mesh):
    return jax.shard_map(
        on_device,
        mesh=mesh,
        in_specs=(
            P(("groups", "row", "tile"), None, None, None),
            P(("groups", "row"), None),
            P("groups"),
        ),
        out_specs=P(("groups", "tile"), "row", None),
        check_vma=False,
    )
```

```python
import functools

import jax
import jax.numpy as jnp
from jax import lax
from jax.experimental import pallas as pl
from jax.experimental.pallas import tpu as pltpu
from jax.sharding import PartitionSpec as P

NB = 512
SPAN = 8
STRIP = 2 * SPAN

SPLIT = (240, 240, 512, 240)
BLOCK = 128
ORDER = (2, 3, 1)
X_FIRST = ((0, 2), (1, 3))
TAIL_CUT = 2
TAIL_ROWS = 208

HBM = pl.BlockSpec(memory_space=pltpu.HBM)
ANY = pl.BlockSpec(memory_space=pl.ANY)
VMEM = pl.BlockSpec(memory_space=pltpu.VMEM)
SMEM = pl.BlockSpec(memory_space=pltpu.SMEM)
PARAMS = pltpu.CompilerParams(vmem_limit_bytes=32 * 1024 * 1024)


def cut(first, last, count):
    edges = [first + (last - first) * at // count // 16 * 16 for at in range(count)] + [last]
    return list(zip(edges, edges[1:]))


def groups_of(first, last):
    return [(low, high - low) for low, high in cut(first, last, -(-(last - first) // BLOCK))]


def early(part):
    made = [[(apart, groups_of(0, SPLIT[apart])) for apart in held if SPLIT[apart] > 0] for held in X_FIRST]
    return [message for message in made if message]


def z_first(part):
    made = []
    for apart in ORDER:
        if SPLIT[apart] < part:
            made.append((apart, groups_of(SPLIT[apart], part)))
    return made


def tail(part):
    middle = SPLIT[0] + TAIL_ROWS
    return [groups_of(SPLIT[0], middle), groups_of(middle, part)]


def message_rows(groups):
    return sum(rows for _, rows in groups) + -(-len(groups) // 16) * 16


def power_of(values):
    top = jnp.max(jnp.abs(values), axis=0, keepdims=True)
    return jnp.ceil(jnp.log2(jnp.maximum(top, 1e-30)))


def widen(codes):
    return codes.astype(jnp.int32).astype(jnp.float32)


def pack(groups, message_ref, tile_ref):
    first = 0
    tile_ref[...] = jnp.zeros_like(tile_ref)
    for at, values in enumerate(groups):
        power = power_of(values)
        codes = jnp.clip(jnp.round(values * jnp.exp2(15.0 - power)), -32767.0, 32767.0)
        message_ref[first : first + values.shape[0], :] = codes.astype(jnp.int32).astype(jnp.int16)
        tile_ref[at : at + 1, :] = power
        first += values.shape[0]
    extra = message_ref.shape[0] - first
    message_ref[first:, :] = tile_ref[0:extra, :].astype(jnp.int32).astype(jnp.int16)


def unpack(message_ref, groups):
    total = sum(rows for _, rows in groups)
    scales = jnp.exp2(widen(message_ref[total:, :]) - 15.0)
    made = []
    first = 0
    for at, (_, rows) in enumerate(groups):
        made.append(widen(message_ref[first : first + rows, :]) * scales[at : at + 1, :])
        first += rows
    return made


def part_rows(owner, first, rows, part):
    return pl.ds(pl.multiple_of(owner * part + first, 16), rows)


def plan_of(cols_ref, low_ref, fields_ref, quota):
    here = lax.axis_index("tile")
    cols = cols_ref[...]
    count = cols.shape[1]
    folded = jnp.minimum(cols, NB - 1 - cols)
    near = (folded == low_ref[here]).astype(jnp.int32)
    far = (folded == low_ref[here ^ 2]).astype(jnp.int32)
    hit = near + far
    target = jnp.sum(hit * cols, axis=0, keepdims=True)
    slot = jnp.sum(hit * lax.broadcasted_iota(jnp.int32, cols.shape, 0), axis=0, keepdims=True)
    local = jnp.sum(near, axis=0, keepdims=True)
    wanted = jnp.sum(hit, axis=0, keepdims=True)
    place = cols - target + SPAN - 1
    good = (cols >= 0) & (place >= 0) & (place < SPAN)
    place = jnp.where(good, place + jnp.where(target >= NB // 2, SPAN, 0), STRIP)
    panel = lax.broadcasted_iota(jnp.int32, (1, count), 1)
    device = panel // (4 * quota)
    mate = (device == (here ^ 1)).astype(jnp.int32)
    wanted = (wanted > 0) & ((device == here) | (mate > 0))
    group = jnp.where(wanted, local * 2 + mate, -1)
    members = (lax.broadcasted_iota(jnp.int32, (8, count), 0) == group).astype(jnp.float32)
    before = (
        lax.broadcasted_iota(jnp.int32, (count, count), 0) < lax.broadcasted_iota(jnp.int32, (count, count), 1)
    ).astype(jnp.float32)
    ranks = jnp.dot(members, before, preferred_element_type=jnp.float32)
    rank = jnp.sum(members * ranks, axis=0, keepdims=True).astype(jnp.int32)
    entry = jnp.where(wanted, group * quota + rank, -1)
    chosen = (lax.broadcasted_iota(jnp.int32, (4 * quota, count), 0) == entry).astype(jnp.float32)
    fields_ref[...] = jnp.zeros_like(fields_ref)
    fields_ref[0:1, 0:count] = (panel % (4 * quota)).astype(jnp.float32)
    fields_ref[1:2, 0:count] = slot.astype(jnp.float32)
    fields_ref[2:6, 0:count] = place.astype(jnp.float32)
    table = lax.dot_general(
        chosen, fields_ref[:, 0:count], (((1,), (1,)), ((), ())), preferred_element_type=jnp.float32
    )
    return table.astype(jnp.int32)


def add_products(plan_ref, entry, panels_ref, sums_ref):
    panel = plan_ref[entry, 0]
    column = panels_ref[panel, plan_ref[entry, 1]].T
    size = column.shape[0]
    wide = jnp.concatenate([panels_ref[panel, slot] for slot in range(4)], axis=1)
    made = jnp.dot(column, wide, preferred_element_type=jnp.float32)
    for slot in range(4):
        place = pl.multiple_of(plan_ref[entry, 2 + slot] * size, size)
        sums_ref[pl.ds(place, size), :] += made[:, slot * size : (slot + 1) * size]


def near_kernel(cols_hbm, low_hbm, blocks_ref, plan_ref, far_ref, own_ref, held, cols_ref, low_ref, fields, table, sems):
    quota = blocks_ref.shape[0] // 4
    cols_copy = pltpu.make_async_copy(cols_hbm, cols_ref, sems.at[0])
    low_copy = pltpu.make_async_copy(low_hbm, low_ref, sems.at[1])
    held_copy = pltpu.make_async_copy(blocks_ref, held, sems.at[2])
    cols_copy.start()
    low_copy.start()
    held_copy.start()
    far_ref[...] = jnp.zeros_like(far_ref)
    own_ref[...] = jnp.zeros_like(own_ref)
    low_copy.wait()
    cols_copy.wait()
    table[:, 0:8] = plan_of(cols_ref, low_ref, fields, quota)
    plan_copy = pltpu.make_async_copy(table, plan_ref, sems.at[3])
    plan_copy.start()
    plan_copy.wait()
    held_copy.wait()
    for at in range(quota):
        add_products(plan_ref, at, held, far_ref)
        add_products(plan_ref, 2 * quota + at, held, own_ref)


def add_mate(plan_ref, mate_ref, far_ref, own_ref):
    quota = mate_ref.shape[0] // 4
    for at in range(quota):
        add_products(plan_ref, quota + at, mate_ref, far_ref)
        add_products(plan_ref, 3 * quota + at, mate_ref, own_ref)


def split_kernel(plan_ref, mate_ref, far_in, own_in, *refs):
    *refs, far_ref, own_ref, tile = refs
    add_mate(plan_ref, mate_ref, far_ref, own_ref)
    here = lax.axis_index("row")
    part = STRIP * far_ref.shape[1] // 4
    for held in early(part):
        groups = [far_ref[part_rows(here ^ apart, *group, part), :] for apart, groups in held for group in groups]
        pack(groups, refs.pop(0), tile)
    for apart, groups in z_first(part):
        groups = [ref[part_rows(here ^ apart, *group, part), :] for ref in (far_ref, own_ref) for group in groups]
        pack(groups, refs.pop(0), tile)


def after_x_kernel(held, after_ref, x_ref, own_ref, *refs):
    *refs, tile = refs
    here = lax.axis_index("row")
    part = STRIP * own_ref.shape[1] // 4
    received = unpack(x_ref, [group for _, groups in held for group in groups])
    for apart, groups in held:
        totals = [own_ref[part_rows(here ^ apart, *group, part), :] + received.pop(0) for group in groups]
        if apart == 0:
            refs[0][...] = jnp.concatenate(totals)
        else:
            pack(totals, refs[0], tile)
        refs = refs[1:]


def after_z_kernel(after_ref, far_ref, own_ref, *refs):
    z_refs, x_refs = refs[: len(refs) - TAIL_CUT - 3], refs[len(refs) - TAIL_CUT - 3 : -3]
    keep_ref, far_sum, tile = refs[-3:]
    here = lax.axis_index("row")
    part = STRIP * own_ref.shape[1] // 4
    first = SPLIT[0]
    for sums_ref, total_ref in ((far_ref, far_sum), (own_ref, keep_ref)):
        total_ref[...] = sums_ref[part_rows(here, first, part - first, part), :]
    for (apart, groups), z_ref in zip(z_first(part), z_refs):
        received = unpack(z_ref, 2 * groups)
        for total_ref in (far_sum, keep_ref):
            for low, rows in groups:
                total_ref[low - first : low - first + rows, :] += received.pop(0)
    for groups, x_ref in zip(tail(part), x_refs):
        pack([far_sum[low - first : low - first + rows, :] for low, rows in groups], x_ref, tile)


def last_kernel(keep_q, keep_p, *refs):
    x_refs, z_refs, out_ref = refs[:TAIL_CUT], refs[TAIL_CUT:-1], refs[-1]
    part, size = out_ref.shape[1:]
    first = SPLIT[0]
    if first > 0:
        out_ref[0, 0:first, :] = keep_p[...]
    for groups, x_ref in zip(tail(part), x_refs):
        for (low, rows), values in zip(groups, unpack(x_ref, groups)):
            out_ref[0, low : low + rows, :] = keep_q[low - first : low - first + rows, :] + values
    came = dict(pair for held in early(part) for pair in held)
    for apart, z_ref in zip([apart for apart in ORDER if apart in came], z_refs):
        for (low, rows), values in zip(came[apart], unpack(z_ref, came[apart])):
            out_ref[0, low : low + rows, :] += values
    row = lax.broadcasted_iota(jnp.int32, (size, size), 0)
    column = lax.broadcasted_iota(jnp.int32, (size, size), 1)
    odd = lax.axis_index("row") % 2 == 1
    out_ref[0, part - size :, :] += jnp.where((row == column) & odd, 1.0, 0.0)


def all_kernel(plan_ref, mate_ref, far_in, own_in, x_ref, far_ref, own_ref, tile):
    add_mate(plan_ref, mate_ref, far_ref, own_ref)
    size = far_ref.shape[1]
    pack([far_ref[low : low + rows, :] for low, rows in groups_of(0, STRIP * size)], x_ref, tile)


def add_kernel(own_ref, x_ref, sum_ref):
    groups = groups_of(0, sum_ref.shape[0])
    for (low, rows), values in zip(groups, unpack(x_ref, groups)):
        sum_ref[low : low + rows, :] = own_ref[low : low + rows, :] + values


def call(kernel, outs, operands, specs, out_specs=None, scratch=(), size=1 << 20, aliases=None):
    return pl.pallas_call(
        kernel,
        out_shape=outs,
        in_specs=specs,
        out_specs=jax.tree.map(lambda _: VMEM, outs) if out_specs is None else out_specs,
        scratch_shapes=list(scratch),
        input_output_aliases=aliases or {},
        compiler_params=PARAMS,
        cost_estimate=pl.CostEstimate(flops=0, bytes_accessed=size, transcendentals=0),
    )(*operands)


def on_device(blocks, block_cols, pair_low):
    panels_here, slots, size, _ = blocks.shape
    tiles_count = lax.axis_size("tile")
    rows_count = lax.axis_size("row")
    assert tiles_count == 4 and pair_low.shape[0] == 4 and slots == 4
    strip_rows = STRIP * size
    share = strip_rows // 4
    assert SPLIT[0] == SPLIT[1] <= min(SPLIT[2:]) and max(SPLIT) <= share

    def swap(value, axis, apart):
        return lax.ppermute(value, axis, [(i, i ^ apart) for i in range(lax.axis_size(axis))])

    def message(groups):
        return jax.ShapeDtypeStruct((message_rows(groups), size), jnp.int16)

    def full(rows):
        return jax.ShapeDtypeStruct((rows, size), jnp.float32)

    mate = swap(blocks, "tile", 1)
    strip = full(strip_rows + size)
    plan, far, own = call(
        near_kernel,
        [pltpu.SMEM((panels_here, 128), jnp.int32), strip, strip],
        tuple(pltpu.with_memory_space_constraint(value, pltpu.HBM) for value in (block_cols.T, pair_low, blocks)),
        [HBM, HBM, HBM],
        [SMEM, VMEM, VMEM],
        [
            pltpu.VMEM(blocks.shape, blocks.dtype),
            pltpu.VMEM(block_cols.shape[::-1], jnp.int32),
            pltpu.SMEM(pair_low.shape, jnp.int32),
            pltpu.VMEM((8, 128), jnp.float32),
            pltpu.VMEM((panels_here, 128), jnp.int32),
            pltpu.SemaphoreType.DMA((4,)),
        ],
        8 << 20,
    )

    tile = pltpu.VMEM((32, size), jnp.float32)

    if rows_count != 4:
        across, far, own = call(
            all_kernel, [message(groups_of(0, strip_rows)), strip, strip], (plan, mate, far, own), [SMEM] + [VMEM] * 3,
            scratch=[tile], aliases={2: 1, 3: 2},
        )
        sums = call(add_kernel, full(strip_rows), (own, swap(across, "tile", 2)), [VMEM, VMEM])
        part = lax.psum_scatter(sums[None], "row", scatter_dimension=1, tiled=True)
        rows = lax.axis_index("row") * part.shape[1] + jnp.arange(part.shape[1], dtype=jnp.int32)
        unit = (rows // size % SPAN == SPAN - 1)[:, None] & ((rows % size)[:, None] == jnp.arange(size)[None, :])
        return part + unit.astype(jnp.float32)[None]

    x_sent, z_sent = early(share), z_first(share)
    x_groups = [[group for _, groups in held for group in groups] for held in x_sent]
    *made, far, own = call(
        split_kernel,
        [*[message(groups) for groups in x_groups], *[message(2 * groups) for _, groups in z_sent], strip, strip],
        (plan, mate, far, own), [SMEM] + [VMEM] * 3, scratch=[tile],
        aliases={2: len(x_sent) + len(z_sent), 3: len(x_sent) + len(z_sent) + 1},
    )
    over_x = [swap(made.pop(0), "tile", 2) for _ in x_sent]
    q_z = [swap(made.pop(0), "row", apart) for apart, _ in z_sent]
    after, second = plan, {}
    for held, value in zip(x_sent, over_x):
        results = [full(SPLIT[0]) if apart == 0 else message(groups) for apart, groups in held]
        results = call(
            functools.partial(after_x_kernel, held), results, (after, value, own), [ANY, VMEM, VMEM], scratch=[tile]
        )
        after = results[0]
        for (apart, _), value in zip(held, results):
            second[apart] = value if apart == 0 else swap(value, "row", apart)
    p_keep = second.get(0, plan)
    p_z = [second[apart] for apart in ORDER if apart in second]
    rest = share - SPLIT[0]
    *q_x, q_keep = call(
        after_z_kernel, [*[message(groups) for groups in tail(share)], full(rest)], (after, far, own, *q_z),
        [ANY] + [VMEM] * (2 + len(q_z)), scratch=[pltpu.VMEM((rest, size), jnp.float32), tile],
    )
    q_x = [swap(value, "tile", 2) for value in q_x]
    out = jax.ShapeDtypeStruct((1, share, size), jnp.float32)
    return call(last_kernel, out, (q_keep, p_keep, *q_x, *p_z), [VMEM, VMEM if 0 in second else ANY] + [VMEM] * (len(q_x) + len(p_z)))


def solution(mesh):
    return jax.shard_map(
        on_device,
        mesh=mesh,
        in_specs=(
            P(("groups", "row", "tile"), None, None, None),
            P(("groups", "row"), None),
            P("groups"),
        ),
        out_specs=P(("groups", "tile"), "row", None),
        check_vma=False,
    )
```
